512 devices in a mesh: section: 4 (over x_lo, core), tm: 8 (over y, x_hi), space: 16 (over z).
Axes of the slice: x: 4 (x_hi: 2, x_lo: 2; x = x_hi * 2 + x_lo), y: 4, z: 16, core: 2. Of those that a mesh axis runs over, the one named last changes fastest.
Arguments:
- hidden_in: bfloat16 [4, 8, 2048, 1152], P('section', 'tm', 'space'), may hold values from -6 to 6
- query_s: bfloat16 [4, 8, 2048, 1152], P('section', 'tm', 'space'), may hold values from -8 to 8
- key_s: bfloat16 [4, 8, 2048, 1152], P('section', 'tm', 'space'), may hold values from -8 to 8
- value_s: bfloat16 [4, 8, 2048, 1152], P('section', 'tm', 'space'), may hold values from -6 to 6
- out_proj_s: bfloat16 [4, 1152, 1152], P('section', 'space'), may hold values from -0.1875 to 0.1875
- gate_s: float32 [4, 1152], P('section'), may hold values from 0.1 to 1.9
- shift_t: float32 [4, 1152], P('section'), may hold values from -3 to 3
- scale_t: float32 [4, 1152], P('section'), may hold values from -3 to 3
- qkv_t: bfloat16 [4, 3, 1152, 1152], P('section', None, 'tm'), may hold values from -0.1875 to 0.1875
- out_t: bfloat16 [4, 1152, 1152], P('section', 'tm'), may hold values from -0.1875 to 0.1875
- gate_t: float32 [4, 1152], P('section'), may hold values from 0.1 to 1.9
Outputs:
- handed: bfloat16 [4, 8, 2048, 1152], P('section', 'tm', 'space')
The draws below stay inside these ranges and needn't reach their ends.
All inputs are finite; a program needn't handle non-finite values.
Results may differ from the reference program's by a relative error of at most 0.022.
Values may be sent and summed in bfloat16 or wider, within the bound.
A program may use at most 64 MiB of HBM per device.

```python
import jax
import jax.numpy as jnp
from jax import lax

D = 1152
HEADS = 16
PATCHES = 2048
FRAMES = 8
SECTIONS = 4


def draw_query_s(key, part):
    key = jax.random.fold_in(key, 11)
    shape = (SECTIONS, FRAMES, PATCHES, D)
    values = jnp.clip(jax.random.normal(key, shape, jnp.float32), -6.0, 6.0)
    return values.astype(jnp.bfloat16)


def draw_key_s(key, part):
    key = jax.random.fold_in(key, 23)
    shape = (SECTIONS, FRAMES, PATCHES, D)
    values = jnp.clip(jax.random.normal(key, shape, jnp.float32), -6.0, 6.0)
    return values.astype(jnp.bfloat16)


def shard_levels(rng, extent, shards, smallest, high):
    factor_of = 1.0
    for dim, parts in shards:
        draws = jax.random.uniform(jax.random.fold_in(jax.random.fold_in(rng, 6), dim), (parts,), jnp.float32, smallest / len(shards), high / len(shards))
        factor_of = factor_of * jnp.repeat(jnp.exp(draws), extent[dim] // parts).reshape((-1,) + (1,) * (len(extent) - 1 - dim))
    return factor_of


def gaussian(key, extent, width, bound, pieces=(), kind=jnp.bfloat16):
    result = width * jax.random.normal(key, extent, jnp.float32)
    if pieces:
        result = result * shard_levels(key, extent, pieces, -0.22, 0.18)
    return jnp.clip(result, -bound, bound).astype(kind)


def setup_inputs(seed: int = 0) -> dict:
    arg_keys = jax.random.split(jax.random.key(seed), 12)
    return {
        "hidden_in": gaussian(arg_keys[0], (SECTIONS, FRAMES, PATCHES, D), 1.0, 6.0, ((0, 4), (1, 8), (2, 16))),
        "query_s": draw_query_s(jax.random.fold_in(arg_keys[11], 71), 0),
        "key_s": draw_key_s(jax.random.fold_in(arg_keys[11], 71), 0),
        "value_s": gaussian(arg_keys[3], (SECTIONS, FRAMES, PATCHES, D), 1.0, 6.0, ((0, 4), (1, 8), (2, 16))),
        "out_proj_s": gaussian(arg_keys[4], (SECTIONS, D, D), D ** -0.5, 0.1875, ((0, 4), (1, 16))),
        "gate_s": jnp.clip(1.0 + 0.18 * jax.random.normal(arg_keys[5], (SECTIONS, D), jnp.float32), 0.1, 1.9),
        "shift_t": gaussian(arg_keys[6], (SECTIONS, D), 0.5, 3.0, ((0, 4),), jnp.float32),
        "scale_t": gaussian(arg_keys[7], (SECTIONS, D), 0.5, 3.0, ((0, 4),), jnp.float32),
        "qkv_t": gaussian(arg_keys[8], (SECTIONS, 3, D, D), D ** -0.5, 0.1875, ((0, 4), (2, 8))),
        "out_t": gaussian(arg_keys[9], (SECTIONS, D, D), D ** -0.5, 0.1875, ((0, 4), (1, 8))),
        "gate_t": jnp.clip(1.0 + 0.18 * jax.random.normal(arg_keys[10], (SECTIONS, D), jnp.float32), 0.1, 1.9),
    }


def round_half(values):
    return lax.optimization_barrier(values.astype(jnp.bfloat16)).astype(jnp.float32)

def frame_attention(queries, keys_all, values_all):
    head_dim = D // HEADS

    def single_head(operands):
        query_head, key_head, value_head = operands
        scores = jnp.dot(query_head, key_head.T, preferred_element_type=jnp.float32) * head_dim ** (-0.5)
        weights = jax.nn.softmax(scores, axis=-1).astype(jnp.bfloat16)
        return jnp.dot(weights, value_head, preferred_element_type=jnp.float32).astype(jnp.bfloat16)

    def split_heads(matrix):
        return jnp.transpose(matrix.reshape(PATCHES, HEADS, head_dim), (1, 0, 2))
    outputs = lax.map(single_head, (split_heads(queries), split_heads(keys_all), split_heads(values_all)))
    return jnp.transpose(outputs, (1, 0, 2)).reshape(PATCHES, D)

def section_block(operands):
    hidden, queries, keys_all, values_all, proj_s, gate_one, shift_one, scale_one, qkv_one, proj_t, gate_two = operands
    head_dim = D // HEADS
    attended = lax.map(lambda triple: frame_attention(triple[0], triple[1], triple[2]), (queries, keys_all, values_all))
    flat = attended.reshape(FRAMES * PATCHES, D)
    projected = jnp.dot(flat, proj_s, preferred_element_type=jnp.float32)
    middle = (hidden.reshape(FRAMES * PATCHES, D).astype(jnp.float32) + gate_one * projected).astype(jnp.bfloat16)
    widened = middle.astype(jnp.float32)
    mean_value = lax.optimization_barrier(jnp.mean(widened, axis=-1, keepdims=True))
    centred = widened - mean_value
    variance = lax.optimization_barrier(jnp.mean(centred * centred, axis=-1, keepdims=True))
    normed = (centred * lax.rsqrt(variance + 1e-06) * (1.0 + scale_one) + shift_one).astype(jnp.bfloat16)
    normed_frames = normed.reshape(FRAMES, PATCHES, D)
    projections = jnp.einsum('fpd,ced->cefp', normed_frames.astype(jnp.float32), qkv_one.astype(jnp.float32))
    projections = round_half(projections).reshape(3, HEADS, head_dim, FRAMES, PATCHES)
    scores = jnp.einsum('hdfp,hdgp->hfgp', projections[0], projections[1]) * head_dim ** (-0.5)
    weights = round_half(jax.nn.softmax(scores, axis=2))
    mixed = jnp.einsum('hfgp,hdgp->hdfp', weights, projections[2]).astype(jnp.bfloat16)
    mixed_flat = mixed.reshape(D, FRAMES * PATCHES)
    summed = jnp.dot(mixed_flat.T, proj_t, preferred_element_type=jnp.float32)
    finished = (middle.astype(jnp.float32) + gate_two * summed).astype(jnp.bfloat16)
    return finished.reshape(FRAMES, PATCHES, D)

def reference(hidden_in, query_s, key_s, value_s, out_proj_s, gate_s, shift_t, scale_t, qkv_t, out_t, gate_t):
    block_out = lax.map(section_block, (hidden_in, query_s, key_s, value_s, out_proj_s, gate_s, shift_t, scale_t, qkv_t, out_t, gate_t))
    return jnp.roll(block_out, 1, axis=0)
```

```python
import jax
import jax.numpy as jnp
from jax import lax
from jax.experimental import pallas as pl
from jax.experimental.pallas import tpu as pltpu
from jax.sharding import PartitionSpec as P

MESH = pl.DeviceIdType.MESH
F32 = jnp.float32
BF16 = jnp.bfloat16
D = 1152
HD = 72
NZ = 16
NT = 8
NS = 4
ROWS = 128
PART = 32
FACTOR = HD ** (-0.5)


def kernel(
    q_ref, k_ref, v_ref, hid_hbm, w_ref, gs_ref, sh_ref, sc_ref, qkv_hbm, ot_hbm, gt_ref,
    out_ref,
    kvs, kvr, qs, qr, osd, orc, wz, wt, wfull, kmat, vmat, ofull, wq, wo, hid, mids, midr, mixt, fins, finr,
    skv, rkv, sq, rq, so, ro, sw, rw, swy, rwy, swx, rwx, sqy, rqy, sm, rm, sf, rf, loc,
):
    sec = lax.axis_index("section")
    t = lax.axis_index("tm")
    z = lax.axis_index("space")
    y = t // 2
    xh = t % 2
    nxt = (sec + 1) % NS
    prv = (sec + NS - 1) % NS
    zr = {"space": (z + 1) % NZ}
    zl = {"space": (z + NZ - 1) % NZ}
    yr = {"tm": (t + 2) % NT}
    yl = {"tm": (t + NT - 2) % NT}
    xo = {"tm": t + 1 - 2 * xh}
    t_yr = (t + 2) % NT
    t_yl = (t + NT - 2) % NT
    t_y2 = (t + 4) % NT
    y_r = (y + 1) % 4
    y_l = (y + 3) % 4
    y_2 = (y + 2) % 4

    def remote(src, dst, s_sem, r_sem, dev):
        return pltpu.make_async_remote_copy(
            src_ref=src, dst_ref=dst, send_sem=s_sem, recv_sem=r_sem, device_id=dev, device_id_type=MESH
        )

    barrier = pltpu.get_barrier_semaphore()

    def greet_z(i, c):
        pl.semaphore_signal(barrier, inc=1, device_id={"space": (z + i) % NZ}, device_id_type=MESH)
        return c

    lax.fori_loop(1, NZ, greet_z, 0)

    def greet_t(i, c):
        pl.semaphore_signal(barrier, inc=1, device_id={"tm": (t + i) % NT}, device_id_type=MESH)
        return c

    lax.fori_loop(1, NT, greet_t, 0)

    def greet_s(i, c):
        pl.semaphore_signal(barrier, inc=1, device_id={"section": nxt, "tm": i}, device_id_type=MESH)
        pl.semaphore_signal(barrier, inc=1, device_id={"section": prv, "tm": i}, device_id_type=MESH)
        return c

    lax.fori_loop(0, NT, greet_s, 0)

    loc_q = pltpu.make_async_copy(qkv_hbm, wq.at[y], loc.at[0])
    loc_o = pltpu.make_async_copy(ot_hbm, wo.at[y], loc.at[1])
    loc_h = pltpu.make_async_copy(hid_hbm, hid, loc.at[2])
    loc_q.start()
    loc_o.start()
    loc_h.start()

    wz[z, 0] = w_ref[:, pl.ds(pl.multiple_of(t * 128, 128), 128)]
    wz[z, 1] = w_ref[:, 1024:1152]
    kt = k_ref[...].astype(F32).T
    vt = v_ref[...].astype(F32).T
    for h in range(NZ):
        kvs[h] = jnp.concatenate([kt[HD * h : HD * (h + 1)], vt[HD * h : HD * (h + 1)]], axis=0).astype(BF16)
    qt = q_ref[...].astype(F32).T
    for h in range(NZ):
        qs[h] = qt[HD * h : HD * (h + 1)].astype(BF16)
    kvr[z] = kvs[z]
    qr[z] = qs[z]

    pl.semaphore_wait(barrier, (NZ - 1) + (NT - 1) + 2 * NT)

    def ring_right(j):
        src = (z + NZ - j) % NZ
        return remote(wz.at[src], wz.at[src], sw.at[0, j], rw.at[0, j], zr)

    def ring_left(j):
        src = (z + j) % NZ
        return remote(wz.at[src], wz.at[src], sw.at[1, j], rw.at[1, j], zl)

    def ring_right_half():
        src = (z + NZ - 7) % NZ
        return remote(wz.at[src, 0], wz.at[src, 0], sw.at[0, 7], rw.at[0, 7], zr)

    def ring_left_half():
        src = (z + 7) % NZ
        return remote(wz.at[src, 1], wz.at[src, 1], sw.at[1, 7], rw.at[1, 7], zl)

    ring_right(0).start()
    ring_left(0).start()

    def wq_send(unit, way):
        dev = yr if way == 0 else yl
        if unit < 3:
            return remote(qkv_hbm.at[unit], wq.at[y, unit], sqy.at[way, unit], rqy.at[way, unit], dev)
        return remote(ot_hbm, wo.at[y], sqy.at[way, 3], rqy.at[way, 3], dev)

    for unit in (0, 1, 2, 3):
        wq_send(unit, 0).start()
        wq_send((unit + 2) % 4, 1).start()

    def kv_copy(i):
        to = (z + i) % NZ
        return remote(kvs.at[to], kvr.at[z], skv.at[i], rkv.at[i], {"space": to})

    def q_copy(i):
        to = (z + i) % NZ
        return remote(qs.at[to], qr.at[z], sq.at[i], rq.at[i], {"space": to})

    def kv_start(i, c):
        kv_copy(NZ - i).start()
        kv_copy(i).start()
        return c

    lax.fori_loop(1, 8, kv_start, 0)
    kv_copy(8).start()

    def q_start(i, c):
        q_copy(i).start()
        q_copy(NZ - i).start()
        return c

    lax.fori_loop(1, 8, q_start, 0)
    q_copy(8).start()

    def ring_step(j, c):
        ring_right(j - 1).wait_recv()
        ring_right(j).start()
        ring_left(j - 1).wait_recv()
        ring_left(j).start()
        return c

    lax.fori_loop(1, 7, ring_step, 0)
    ring_right(6).wait_recv()
    ring_right_half().start()
    ring_left(6).wait_recv()
    ring_left_half().start()
    ring_right_half().wait_recv()
    ring_left_half().wait_recv()

    wt[t] = wz[:, 0]

    def wy_copy(way):
        return remote(wt.at[t], wt.at[t], swy.at[way], rwy.at[way], yr if way == 0 else yl)

    def wx_copy(i, tt):
        return remote(wt.at[tt], wt.at[tt], swx.at[i], rwx.at[i], xo)

    wy_copy(0).start()
    wy_copy(1).start()
    wx_copy(0, t).start()

    def take_kv(src):
        block = kvr[src].astype(F32)
        off = pl.ds(pl.multiple_of(src * ROWS, ROWS), ROWS)
        kmat[off, :] = block[:HD].T.astype(BF16)
        vmat[:HD, off] = block[HD:].astype(BF16)

    vmat[HD:, :] = jnp.ones((8, NZ * ROWS), BF16)
    take_kv(z)

    def kv_take(i, c):
        kv_copy(i).wait_recv()
        take_kv((z + NZ - i) % NZ)
        return c

    lax.fori_loop(1, NZ, kv_take, 0)

    def wq_pass(unit, way):
        dev, yy = (yr, y_l) if way == 0 else (yl, y_r)
        if unit < 3:
            return remote(wq.at[yy, unit], wq.at[yy, unit], sqy.at[way, 4 + unit], rqy.at[way, 4 + unit], dev)
        return remote(wo.at[yy], wo.at[yy], sqy.at[way, 7], rqy.at[way, 7], dev)

    def wy_pass(way):
        dev, tt = (yr, t_yl) if way == 0 else (yl, t_yr)
        part = wt.at[tt, pl.ds(8 * way, 8)]
        return remote(part, part, swy.at[2 + way], rwy.at[2 + way], dev)

    wy_copy(0).wait_recv()
    wy_pass(0).start()
    wx_copy(1, t_yl).start()
    wy_copy(1).wait_recv()
    wy_pass(1).start()
    wx_copy(2, t_yr).start()
    for unit, way in ((0, 0), (2, 1), (1, 0), (3, 1)):
        wq_send(unit, way).wait_recv()
        wq_pass(unit, way).start()

    def o_copy(i):
        to = (z + i) % NZ
        return remote(osd.at[to], orc.at[z], so.at[i], ro.at[i], {"space": to})

    def attend(d, c):
        src_a = (z + NZ - d) % NZ
        src_b = jnp.where(d == 8, z, (z + d) % NZ)
        q_copy(d).wait_recv()

        @pl.when(d < 8)
        def _():
            q_copy(NZ - d).wait_recv()

        queries = jnp.concatenate([qr[src_a], qr[src_b]], axis=1)
        s = jnp.dot(kmat[...], queries, preferred_element_type=F32)
        top = jnp.max(s, axis=0, keepdims=True)
        p = jnp.exp((s - top) * FACTOR).astype(BF16)
        o = jnp.dot(vmat[...], p, preferred_element_type=F32)
        o = (o[:HD] / o[HD : HD + 1]).astype(BF16)
        osd[src_a] = o[:, :ROWS]
        osd[src_b] = o[:, ROWS:]
        o_copy(NZ - d).start()

        @pl.when(d < 8)
        def _():
            o_copy(d).start()

        @pl.when(d == 4)
        def _():
            wy_pass(0).wait_recv()
            wy_pass(1).wait_recv()
            wx_copy(3, t_y2).start()

        return c

    lax.fori_loop(1, 9, attend, 0)
    orc[z] = osd[z]

    for i, tt in ((0, t), (1, t_yl), (2, t_yr), (3, t_y2)):
        wx_copy(i, tt).wait_recv()

    def w_rows(j, c):
        row = pl.ds(pl.multiple_of(144 * j, 144), 144)
        for b in range(9):
            if b < 8:
                lo, hi = wt[b, 2 * j], wt[b, 2 * j + 1]
            else:
                lo, hi = wz[2 * j, 1], wz[2 * j + 1, 1]
            wfull[row, 128 * b : 128 * (b + 1)] = jnp.concatenate([lo.astype(F32), hi.astype(F32)], axis=0).astype(BF16)
        return c

    lax.fori_loop(0, 8, w_rows, 0)
    loc_h.wait()

    def o_take(i, c):
        o_copy(i).wait_recv()
        src = (z + NZ - i) % NZ
        ofull[pl.ds(pl.multiple_of(src * HD, 8), HD), :] = orc[src].astype(F32)
        return c

    ofull[pl.ds(pl.multiple_of(z * HD, 8), HD), :] = orc[z].astype(F32)
    lax.fori_loop(1, NZ, o_take, 0)
    attended = ofull[...].T.astype(BF16)
    projected = jnp.dot(attended, wfull[...], preferred_element_type=F32)
    mids[...] = (hid[...].astype(F32) + gs_ref[...] * projected).astype(BF16)

    def mid_copy(i):
        to = (t + i) % NT
        rows = pl.ds(pl.multiple_of((to // 2) * PART, PART), PART)
        return remote(mids.at[rows], midr.at[t], sm.at[i], rm.at[i], {"tm": to})

    def mid_start(i, c):
        mid_copy(i).start()
        return c

    lax.fori_loop(1, NT, mid_start, 0)
    midr[t] = mids[pl.ds(pl.multiple_of(y * PART, PART), PART), :]

    loc_q.wait()
    loc_o.wait()
    for unit, way in ((2, 0), (3, 0), (0, 1), (1, 1)):
        wq_send(unit, way).wait_recv()
    for unit, way in ((0, 0), (2, 1), (1, 0), (3, 1)):
        wq_pass(unit, way).wait_recv()

    def mid_wait(i, c):
        mid_copy(i).wait_recv()
        return c

    lax.fori_loop(1, NT, mid_wait, 0)
    middle = midr[...].reshape(NT * PART, D).astype(F32)
    centred = middle - jnp.mean(middle, axis=-1, keepdims=True)
    variance = jnp.mean(centred * centred, axis=-1, keepdims=True)
    normed = (centred * lax.rsqrt(variance + 1e-06) * (1.0 + sc_ref[...]) + sh_ref[...]).astype(BF16)

    tokens = NT * PART
    same = (lax.broadcasted_iota(jnp.int32, (tokens, tokens), 0) % PART) == (
        lax.broadcasted_iota(jnp.int32, (tokens, tokens), 1) % PART
    )

    def heads(j, c):
        proj = lax.dot_general(
            wq[j].reshape(3 * 144, D), normed, (((1,), (1,)), ((), ())), preferred_element_type=F32
        )
        for e in range(2):
            tq = proj[HD * e : HD * (e + 1)].astype(BF16)
            tk = proj[144 + HD * e : 144 + HD * (e + 1)].T.astype(BF16)
            tv = proj[288 + HD * e : 288 + HD * (e + 1)].astype(BF16)
            s = jnp.dot(tk, tq, preferred_element_type=F32) * FACTOR
            s = jnp.where(same, s, -jnp.inf)
            p = jnp.exp(s - jnp.max(s, axis=0, keepdims=True))
            p = (p / jnp.sum(p, axis=0, keepdims=True)).astype(BF16)
            mixt[pl.ds(pl.multiple_of(144 * j + HD * e, 8), HD), :] = jnp.dot(tv, p, preferred_element_type=F32)
        return c

    lax.fori_loop(0, 4, heads, 0)
    mixed = mixt[...].T.astype(BF16)
    summed = jnp.dot(mixed, wo[...].reshape(576, D), preferred_element_type=F32)
    keep = jnp.where(xh == 0, 1.0, 0.0).astype(F32)
    part = keep * midr[...].reshape(tokens, D).astype(F32) + gt_ref[...] * summed
    fins[...] = part.astype(BF16).reshape(NT, PART, D)

    def fin_copy(f):
        return remote(fins.at[f], finr.at[t], sf.at[f], rf.at[t], {"section": nxt, "tm": f})

    def fin_start(f, c):
        fin_copy(f).start()
        return c

    lax.fori_loop(0, NT, fin_start, 0)

    def fin_wait(f, c):
        remote(fins.at[f], finr.at[f], sf.at[f], rf.at[f], {"section": nxt, "tm": f}).wait_recv()
        return c

    lax.fori_loop(0, NT, fin_wait, 0)
    for j in range(4):
        out_ref[PART * j : PART * (j + 1), :] = (finr[2 * j].astype(F32) + finr[2 * j + 1].astype(F32)).astype(BF16)

    def left_z(i, c):
        kv_copy(i).wait_send()
        q_copy(i).wait_send()
        o_copy(i).wait_send()
        return c

    lax.fori_loop(1, NZ, left_z, 0)

    def left_ring(j, c):
        ring_right(j).wait_send()
        ring_left(j).wait_send()
        return c

    lax.fori_loop(0, 7, left_ring, 0)
    ring_right_half().wait_send()
    ring_left_half().wait_send()
    for way in range(2):
        wy_copy(way).wait_send()
        wy_pass(way).wait_send()
        for unit in range(4):
            wq_send(unit, way).wait_send()
    for i, tt in ((0, t), (1, t_yl), (2, t_yr), (3, t_y2)):
        wx_copy(i, tt).wait_send()
    for unit, way in ((0, 0), (2, 1), (1, 0), (3, 1)):
        wq_pass(unit, way).wait_send()

    def left_t(i, c):
        mid_copy(i).wait_send()
        return c

    lax.fori_loop(1, NT, left_t, 0)

    def left_f(f, c):
        fin_copy(f).wait_send()
        return c

    lax.fori_loop(0, NT, left_f, 0)


def shards(
    hidden_in, query_s, key_s, value_s, out_proj_s, gate_s, shift_t, scale_t, qkv_t, out_t, gate_t
):
    vm = pl.BlockSpec(memory_space=pltpu.VMEM)
    hbm = pl.BlockSpec(memory_space=pl.ANY)
    dma = pltpu.SemaphoreType.DMA
    plane = (HD, ROWS)
    out = pl.pallas_call(
        kernel,
        out_shape=jax.ShapeDtypeStruct((ROWS, D), BF16),
        in_specs=[vm, vm, vm, hbm, vm, vm, vm, vm, hbm, hbm, vm],
        out_specs=vm,
        scratch_shapes=[
            pltpu.VMEM((NZ, 2 * HD, ROWS), BF16),
            pltpu.VMEM((NZ, 2 * HD, ROWS), BF16),
            pltpu.VMEM((NZ, *plane), BF16),
            pltpu.VMEM((NZ, *plane), BF16),
            pltpu.VMEM((NZ, *plane), BF16),
            pltpu.VMEM((NZ, *plane), BF16),
            pltpu.VMEM((NZ, 2, *plane), BF16),
            pltpu.VMEM((NT, NZ, *plane), BF16),
            pltpu.VMEM((D, D), BF16),
            pltpu.VMEM((NZ * ROWS, HD), BF16),
            pltpu.VMEM((HD + 8, NZ * ROWS), BF16),
            pltpu.VMEM((D, ROWS), F32),
            pltpu.VMEM((4, 3, 144, D), BF16),
            pltpu.VMEM((4, 144, D), BF16),
            pltpu.VMEM((ROWS, D), BF16),
            pltpu.VMEM((ROWS, D), BF16),
            pltpu.VMEM((NT, PART, D), BF16),
            pltpu.VMEM((576, NT * PART), F32),
            pltpu.VMEM((NT, PART, D), BF16),
            pltpu.VMEM((NT, PART, D), BF16),
            dma((NZ,)), dma((NZ,)), dma((NZ,)), dma((NZ,)), dma((NZ,)), dma((NZ,)),
            dma((2, 8)), dma((2, 8)), dma((4,)), dma((4,)), dma((4,)), dma((4,)),
            dma((2, 8)), dma((2, 8)), dma((NT,)), dma((NT,)), dma((NT,)), dma((NT,)), dma((3,)),
        ],
        compiler_params=pltpu.CompilerParams(
            collective_id=0, has_side_effects=True, vmem_limit_bytes=56 * 1024 * 1024
        ),
        cost_estimate=pl.CostEstimate(flops=3_000_000_000, bytes_accessed=6_000_000, transcendentals=4_500_000),
        name="st_block_pair",
    )(
        query_s[0, 0], key_s[0, 0], value_s[0, 0], hidden_in[0, 0], out_proj_s[0],
        gate_s, shift_t, scale_t, qkv_t[0], out_t[0], gate_t,
    )
    return out[None, None]


def solution(mesh):
    in_specs = (
        P("section", "tm", "space", None),
        P("section", "tm", "space", None),
        P("section", "tm", "space", None),
        P("section", "tm", "space", None),
        P("section", "space", None),
        P("section", None),
        P("section", None),
        P("section", None),
        P("section", None, "tm", None),
        P("section", "tm", None),
        P("section", None),
    )
    out_specs = P("section", "tm", "space", None)
    return jax.shard_map(shards, mesh=mesh, in_specs=in_specs, out_specs=out_specs, check_vma=False)
```

```python
import jax
import jax.numpy as jnp
from jax import lax
from jax.experimental import pallas as pl
from jax.experimental.pallas import tpu as pltpu
from jax.sharding import PartitionSpec as P

MESH = pl.DeviceIdType.MESH
F32 = jnp.float32
BF16 = jnp.bfloat16
D = 1152
HD = 72
NZ = 16
NT = 8
NS = 4
ROWS = 128
PART = 32
FACTOR = HD ** (-0.5)
FACTOR2 = FACTOR * 1.4426950408889634


def kernel(
    q_hbm, k_hbm, v_hbm, hid_hbm, w_hbm, gs_ref, sh_ref, sc_ref, qkv_hbm, ot_hbm, gt_ref,
    finr,
    q_ref, k_ref, v_ref, w_ref, kvs, kvr, qs, qr, osd, orc, wz, wall, acc, kmat, vmat, wq, wo, hid, mids, midr, mixt, fins,
    skv, rkv, sq, rq, so, ro, sw, rw, swy, rwy, swx, rwx, sqy, rqy, sm, rm, sf, rf, loc,
):
    sec = lax.axis_index("section")
    t = lax.axis_index("tm")
    z = lax.axis_index("space")
    y = t // 2
    xh = t % 2
    nxt = (sec + 1) % NS
    prv = (sec + NS - 1) % NS
    zr = {"space": (z + 1) % NZ}
    zl = {"space": (z + NZ - 1) % NZ}
    yr = {"tm": (t + 2) % NT}
    yl = {"tm": (t + NT - 2) % NT}
    xo = {"tm": t + 1 - 2 * xh}
    t_yr = (t + 2) % NT
    t_yl = (t + NT - 2) % NT
    t_y2 = (t + 4) % NT
    y_r = (y + 1) % 4
    y_l = (y + 3) % 4
    y_2 = (y + 2) % 4

    def remote(src, dst, s_sem, r_sem, dev):
        return pltpu.make_async_remote_copy(
            src_ref=src, dst_ref=dst, send_sem=s_sem, recv_sem=r_sem, device_id=dev, device_id_type=MESH
        )

    barrier = pltpu.get_barrier_semaphore()

    def greet_z(i, c):
        pl.semaphore_signal(barrier, inc=1, device_id={"space": (z + i) % NZ}, device_id_type=MESH)
        return c

    lax.fori_loop(1, NZ, greet_z, 0)

    def greet_t(i, c):
        pl.semaphore_signal(barrier, inc=1, device_id={"tm": (t + i) % NT}, device_id_type=MESH)
        return c

    lax.fori_loop(1, NT, greet_t, 0)

    def greet_s(i, c):
        pl.semaphore_signal(barrier, inc=1, device_id={"section": nxt, "tm": i}, device_id_type=MESH)
        pl.semaphore_signal(barrier, inc=1, device_id={"section": prv, "tm": i}, device_id_type=MESH)
        return c

    lax.fori_loop(0, NT, greet_s, 0)

    loc_in = [
        pltpu.make_async_copy(a, b, loc.at[3 + i])
        for i, (a, b) in enumerate(((k_hbm, k_ref), (v_hbm, v_ref), (q_hbm, q_ref), (w_hbm, w_ref)))
    ]
    for c in loc_in:
        c.start()
    loc_q = pltpu.make_async_copy(qkv_hbm, wq.at[y], loc.at[0])
    loc_o = pltpu.make_async_copy(ot_hbm, wo.at[y], loc.at[1])
    loc_h = pltpu.make_async_copy(hid_hbm, hid, loc.at[2])
    loc_q.start()
    loc_o.start()
    loc_h.start()

    for c in loc_in:
        c.wait()
    wz[z, 0] = w_ref[:, pl.ds(pl.multiple_of(t * 128, 128), 128)]
    wz[z, 1] = w_ref[:, 1024:1152]
    kt = k_ref[...].astype(F32).T
    vt = v_ref[...].astype(F32).T
    for h in range(NZ):
        kvs[h] = jnp.concatenate([kt[HD * h : HD * (h + 1)], vt[HD * h : HD * (h + 1)]], axis=0).astype(BF16)
    qt = q_ref[...].astype(F32).T
    for h in range(NZ):
        qs[h] = qt[HD * h : HD * (h + 1)].astype(BF16)
    kvr[z] = kvs[z]
    qr[z] = qs[z]

    pl.semaphore_wait(barrier, (NZ - 1) + (NT - 1) + 2 * NT)

    def ring_right(j):
        src = (z + NZ - j) % NZ
        return remote(wz.at[src], wz.at[src], sw.at[0, j], rw.at[0, j], zr)

    def ring_left(j):
        src = (z + j) % NZ
        return remote(wz.at[src], wz.at[src], sw.at[1, j], rw.at[1, j], zl)

    def ring_right_half():
        src = (z + NZ - 7) % NZ
        return remote(wz.at[src, 0], wz.at[src, 0], sw.at[0, 7], rw.at[0, 7], zr)

    def ring_left_half():
        src = (z + 7) % NZ
        return remote(wz.at[src, 1], wz.at[src, 1], sw.at[1, 7], rw.at[1, 7], zl)

    ring_right(0).start()
    ring_left(0).start()

    def wq_send(unit, way):
        dev = yr if way == 0 else yl
        if unit < 3:
            return remote(qkv_hbm.at[unit], wq.at[y, unit], sqy.at[way, unit], rqy.at[way, unit], dev)
        return remote(ot_hbm, wo.at[y], sqy.at[way, 3], rqy.at[way, 3], dev)

    for unit in (0, 1, 2, 3):
        wq_send(unit, 0).start()
        wq_send((unit + 2) % 4, 1).start()

    def kv_copy(i):
        to = (z + i) % NZ
        return remote(kvs.at[to], kvr.at[z], skv.at[i], rkv.at[i], {"space": to})

    def q_copy(i):
        to = (z + i) % NZ
        return remote(qs.at[to], qr.at[z], sq.at[i], rq.at[i], {"space": to})

    def kv_start(i):
        kv_copy(NZ - i).start()
        kv_copy(i).start()

    def q_start(i):
        q_copy(i).start()
        q_copy(NZ - i).start()

    def take_kv(src):
        block = kvr[src].astype(F32)
        off = pl.ds(pl.multiple_of(src * ROWS, ROWS), ROWS)
        kmat[off, :] = block[:HD].T.astype(BF16)
        vmat[:HD, off] = block[HD:].astype(BF16)

    def kv_take(i, c):
        kv_copy(i).wait_recv()
        take_kv((z + NZ - i) % NZ)
        kv_copy(NZ - i).wait_recv()
        take_kv((z + i) % NZ)
        return c

    kv_start(1)
    kv_start(2)
    kv_start(3)
    vmat[HD:, :] = jnp.ones((8, NZ * ROWS), BF16)
    take_kv(z)
    for j in range(1, 7):
        if j < 5:
            kv_start(j + 3)
        elif j == 5:
            kv_copy(8).start()
            q_start(1)
        else:
            q_start(2)
            q_start(3)
        ring_right(j - 1).wait_recv()
        ring_right(j).start()
        ring_left(j - 1).wait_recv()
        ring_left(j).start()
        if j > 2:
            kv_take(j - 2, 0)
    ring_right(6).wait_recv()
    ring_right_half().start()
    ring_left(6).wait_recv()
    ring_left_half().start()
    q_start(4)
    q_start(5)
    ring_right_half().wait_recv()
    ring_left_half().wait_recv()

    def columns(tt):
        return wall.at[:, :, pl.ds(pl.multiple_of(tt * 128, 128), 128)]

    wall[:, :, pl.ds(pl.multiple_of(t * 128, 128), 128)] = wz[:, 0]
    wall[:, :, 1024:1152] = wz[:, 1]

    def wy_copy(way):
        return remote(columns(t), columns(t), swy.at[way], rwy.at[way], yr if way == 0 else yl)

    def wx_copy(i, tt):
        return remote(columns(tt), columns(tt), swx.at[i], rwx.at[i], xo)

    wy_copy(0).start()
    wy_copy(1).start()
    wx_copy(0, t).start()
    q_start(6)
    q_start(7)
    q_copy(8).start()

    lax.fori_loop(5, 8, kv_take, 0)
    kv_copy(8).wait_recv()
    take_kv((z + 8) % NZ)

    def wq_pass(unit, way):
        dev, yy = (yr, y_l) if way == 0 else (yl, y_r)
        if unit < 3:
            return remote(wq.at[yy, unit], wq.at[yy, unit], sqy.at[way, 4 + unit], rqy.at[way, 4 + unit], dev)
        return remote(wo.at[yy], wo.at[yy], sqy.at[way, 7], rqy.at[way, 7], dev)

    def wy_pass(way):
        dev, tt = (yr, t_yl) if way == 0 else (yl, t_yr)
        part = wall.at[pl.ds(8 * way, 8), :, pl.ds(pl.multiple_of(tt * 128, 128), 128)]
        return remote(part, part, swy.at[2 + way], rwy.at[2 + way], dev)

    wy_copy(0).wait_recv()
    wy_pass(0).start()
    wx_copy(1, t_yl).start()
    wy_copy(1).wait_recv()
    wy_pass(1).start()
    wx_copy(2, t_yr).start()
    for unit, way in ((0, 0), (2, 1), (1, 0), (3, 1)):
        wq_send(unit, way).wait_recv()
        wq_pass(unit, way).start()

    def o_copy(i):
        to = (z + i) % NZ
        return remote(osd.at[to], orc.at[z], so.at[i], ro.at[i], {"space": to})

    def attend(d, c):
        src_a = (z + NZ - d) % NZ
        src_b = jnp.where(d == 8, z, (z + d) % NZ)
        q_copy(d).wait_recv()

        @pl.when(d < 8)
        def _():
            q_copy(NZ - d).wait_recv()

        queries = jnp.concatenate([qr[src_a], qr[src_b]], axis=1)
        s = jnp.dot(kmat[...], queries, preferred_element_type=F32)
        top = jnp.max(s, axis=0, keepdims=True)
        p = jnp.exp2((s - top) * FACTOR2).astype(BF16)
        o = jnp.dot(vmat[...], p, preferred_element_type=F32)
        o = (o[:HD] / o[HD : HD + 1]).astype(BF16)
        osd[src_a] = o[:, :ROWS]
        osd[src_b] = o[:, ROWS:]
        o_copy(NZ - d).start()

        @pl.when(d < 8)
        def _():
            o_copy(d).start()

        @pl.when(d == 4)
        def _():
            wy_pass(0).wait_recv()
            wy_pass(1).wait_recv()
            wx_copy(3, t_y2).start()

        return c

    lax.fori_loop(1, 9, attend, 0)
    orc[z] = osd[z]

    for i, tt in ((0, t), (1, t_yl), (2, t_yr), (3, t_y2)):
        wx_copy(i, tt).wait_recv()

    def project(src):
        return jnp.dot(orc[src].astype(F32).T.astype(BF16), wall[src], preferred_element_type=F32)

    def o_take(d, c):
        o_copy(d).wait_recv()
        o_copy(NZ - d).wait_recv()
        acc[...] += project((z + NZ - d) % NZ) + project((z + d) % NZ)
        return c

    acc[...] = project(z)
    lax.fori_loop(1, 8, o_take, 0)
    o_copy(8).wait_recv()
    loc_h.wait()
    projected = acc[...] + project((z + 8) % NZ)
    mids[...] = (hid[...].astype(F32) + gs_ref[...] * projected).astype(BF16)

    def mid_copy(i):
        to = (t + i) % NT
        rows = pl.ds(pl.multiple_of((to // 2) * PART, PART), PART)
        return remote(mids.at[rows], midr.at[t], sm.at[i], rm.at[i], {"tm": to})

    def mid_start(i, c):
        mid_copy(i).start()
        return c

    lax.fori_loop(1, NT, mid_start, 0)
    midr[t] = mids[pl.ds(pl.multiple_of(y * PART, PART), PART), :]

    loc_q.wait()
    loc_o.wait()
    for unit, way in ((2, 0), (3, 0), (0, 1), (1, 1)):
        wq_send(unit, way).wait_recv()
    for unit, way in ((0, 0), (2, 1), (1, 0), (3, 1)):
        wq_pass(unit, way).wait_recv()

    def mid_wait(i, c):
        mid_copy(i).wait_recv()
        return c

    lax.fori_loop(1, NT, mid_wait, 0)
    middle = midr[...].reshape(NT * PART, D).astype(F32)
    centred = middle - jnp.mean(middle, axis=-1, keepdims=True)
    variance = jnp.mean(centred * centred, axis=-1, keepdims=True)
    normed = (centred * lax.rsqrt(variance + 1e-06) * (1.0 + sc_ref[...]) + sh_ref[...]).astype(BF16)

    tokens = NT * PART
    same = (lax.broadcasted_iota(jnp.int32, (tokens, tokens), 0) % PART) == (
        lax.broadcasted_iota(jnp.int32, (tokens, tokens), 1) % PART
    )

    def heads(j, c):
        proj = lax.dot_general(
            wq[j].reshape(3 * 144, D), normed, (((1,), (1,)), ((), ())), preferred_element_type=F32
        )
        for e in range(2):
            tq = proj[HD * e : HD * (e + 1)].astype(BF16)
            tk = proj[144 + HD * e : 144 + HD * (e + 1)].T.astype(BF16)
            tv = proj[288 + HD * e : 288 + HD * (e + 1)].astype(BF16)
            s = jnp.dot(tk, tq, preferred_element_type=F32) * FACTOR
            s = jnp.where(same, s, -jnp.inf)
            p = jnp.exp(s - jnp.max(s, axis=0, keepdims=True))
            p = (p / jnp.sum(p, axis=0, keepdims=True)).astype(BF16)
            mixt[pl.ds(pl.multiple_of(144 * j + HD * e, 8), HD), :] = jnp.dot(tv, p, preferred_element_type=F32)
        return c

    lax.fori_loop(0, 4, heads, 0)
    mixed = mixt[...].T.astype(BF16)
    keep = jnp.where(xh == 0, 1.0, 0.0).astype(F32)

    def fin_copy(f):
        return remote(fins.at[f], finr.at[t], sf.at[f], rf.at[t], {"section": nxt, "tm": f})

    for half in range(2):
        rows = slice(128 * half, 128 * (half + 1))
        summed = jnp.dot(mixed[rows], wo[...].reshape(576, D), preferred_element_type=F32)
        part = keep * midr[4 * half : 4 * (half + 1)].reshape(128, D).astype(F32) + gt_ref[...] * summed
        fins[4 * half : 4 * (half + 1)] = part.astype(BF16).reshape(4, PART, D)
        for f in range(4 * half, 4 * (half + 1)):
            fin_copy(f).start()

    def fin_wait(f, c):
        remote(fins.at[f], finr.at[f], sf.at[f], rf.at[f], {"section": nxt, "tm": f}).wait_recv()
        return c

    lax.fori_loop(0, NT, fin_wait, 0)
    def left_z(i, c):
        kv_copy(i).wait_send()
        q_copy(i).wait_send()
        o_copy(i).wait_send()
        return c

    lax.fori_loop(1, NZ, left_z, 0)

    def left_ring(j, c):
        ring_right(j).wait_send()
        ring_left(j).wait_send()
        return c

    lax.fori_loop(0, 7, left_ring, 0)
    ring_right_half().wait_send()
    ring_left_half().wait_send()
    for way in range(2):
        wy_copy(way).wait_send()
        wy_pass(way).wait_send()
        for unit in range(4):
            wq_send(unit, way).wait_send()
    for i, tt in ((0, t), (1, t_yl), (2, t_yr), (3, t_y2)):
        wx_copy(i, tt).wait_send()
    for unit, way in ((0, 0), (2, 1), (1, 0), (3, 1)):
        wq_pass(unit, way).wait_send()

    def left_t(i, c):
        mid_copy(i).wait_send()
        return c

    lax.fori_loop(1, NT, left_t, 0)

    def left_f(f, c):
        fin_copy(f).wait_send()
        return c

    lax.fori_loop(0, NT, left_f, 0)


def shards(
    hidden_in, query_s, key_s, value_s, out_proj_s, gate_s, shift_t, scale_t, qkv_t, out_t, gate_t
):
    vm = pl.BlockSpec(memory_space=pltpu.VMEM)
    hbm = pl.BlockSpec(memory_space=pl.ANY)
    dma = pltpu.SemaphoreType.DMA
    plane = (HD, ROWS)
    out = pl.pallas_call(
        kernel,
        out_shape=jax.ShapeDtypeStruct((NT, PART, D), BF16),
        in_specs=[hbm, hbm, hbm, hbm, hbm, vm, vm, vm, hbm, hbm, vm],
        out_specs=hbm,
        scratch_shapes=[
            pltpu.VMEM((ROWS, D), BF16),
            pltpu.VMEM((ROWS, D), BF16),
            pltpu.VMEM((ROWS, D), BF16),
            pltpu.VMEM((HD, D), BF16),
            pltpu.VMEM((NZ, 2 * HD, ROWS), BF16),
            pltpu.VMEM((NZ, 2 * HD, ROWS), BF16),
            pltpu.VMEM((NZ, *plane), BF16),
            pltpu.VMEM((NZ, *plane), BF16),
            pltpu.VMEM((NZ, *plane), BF16),
            pltpu.VMEM((NZ, *plane), BF16),
            pltpu.VMEM((NZ, 2, *plane), BF16),
            pltpu.VMEM((NZ, HD, D), BF16),
            pltpu.VMEM((ROWS, D), F32),
            pltpu.VMEM((NZ * ROWS, HD), BF16),
            pltpu.VMEM((HD + 8, NZ * ROWS), BF16),
            pltpu.VMEM((4, 3, 144, D), BF16),
            pltpu.VMEM((4, 144, D), BF16),
            pltpu.VMEM((ROWS, D), BF16),
            pltpu.VMEM((ROWS, D), BF16),
            pltpu.VMEM((NT, PART, D), BF16),
            pltpu.VMEM((576, NT * PART), F32),
            pltpu.VMEM((NT, PART, D), BF16),
            dma((NZ,)), dma((NZ,)), dma((NZ,)), dma((NZ,)), dma((NZ,)), dma((NZ,)),
            dma((2, 8)), dma((2, 8)), dma((4,)), dma((4,)), dma((4,)), dma((4,)),
            dma((2, 8)), dma((2, 8)), dma((NT,)), dma((NT,)), dma((NT,)), dma((NT,)), dma((7,)),
        ],
        compiler_params=pltpu.CompilerParams(
            collective_id=0, has_side_effects=True, vmem_limit_bytes=56 * 1024 * 1024
        ),
        cost_estimate=pl.CostEstimate(flops=3_000_000_000, bytes_accessed=6_000_000, transcendentals=4_500_000),
        name="st_block_pair",
    )(
        query_s[0, 0], key_s[0, 0], value_s[0, 0], hidden_in[0, 0], out_proj_s[0],
        gate_s, shift_t, scale_t, qkv_t[0], out_t[0], gate_t,
    )
    halves = out.reshape(4, 2, PART, D).astype(F32)
    return (halves[:, 0] + halves[:, 1]).astype(BF16).reshape(1, 1, ROWS, D)


def solution(mesh):
    in_specs = (
        P("section", "tm", "space", None),
        P("section", "tm", "space", None),
        P("section", "tm", "space", None),
        P("section", "tm", "space", None),
        P("section", "space", None),
        P("section", None),
        P("section", None),
        P("section", None),
        P("section", None, "tm", None),
        P("section", "tm", None),
        P("section", None),
    )
    out_specs = P("section", "tm", "space", None)
    return jax.shard_map(shards, mesh=mesh, in_specs=in_specs, out_specs=out_specs, check_vma=False)
```

```python
import jax
import jax.numpy as jnp
from jax import lax
from jax.experimental import pallas as pl
from jax.experimental.pallas import tpu as pltpu
from jax.sharding import PartitionSpec as P

MESH = pl.DeviceIdType.MESH
F32 = jnp.float32
BF16 = jnp.bfloat16
D = 1152
HD = 72
NZ = 16
NT = 8
NS = 4
ROWS = 128
PART = 32
HALF = 16
PACE = (2, 1)
KV1 = 5
FACTOR = HD ** (-0.5)
FACTOR2 = FACTOR * 1.4426950408889634


def kernel(
    q_hbm, k_hbm, v_hbm, hid_hbm, w_hbm, gs_ref, sh_ref, sc_ref, qkv_hbm, ot_hbm, gt_ref,
    finr,
    q_ref, k_ref, v_ref, w_ref, kvs, kvr, qs, qr, osd, orc, wpad, ws, wall, acc, kmat, vmat, wq, wo, hid, mids, midr, proj, mixt, fins,
    skv, rkv, sq, rq, so, ro, swz, rwz, swy, rwy, swx, rwx, sqy, rqy, sm, rm, sf, rf, loc,
):
    sec = lax.axis_index("section")
    t = lax.axis_index("tm")
    z = lax.axis_index("space")
    y = t // 2
    xh = t % 2
    nxt = (sec + 1) % NS
    prv = (sec + NS - 1) % NS
    zr = {"space": (z + 1) % NZ}
    zl = {"space": (z + NZ - 1) % NZ}
    yr = {"tm": (t + 2) % NT}
    yl = {"tm": (t + NT - 2) % NT}
    xo = {"tm": t + 1 - 2 * xh}
    t_yr = (t + 2) % NT
    t_yl = (t + NT - 2) % NT
    t_y2 = (t + 4) % NT
    y_r = (y + 1) % 4
    y_l = (y + 3) % 4

    def remote(src, dst, s_sem, r_sem, dev):
        return pltpu.make_async_remote_copy(
            src_ref=src, dst_ref=dst, send_sem=s_sem, recv_sem=r_sem, device_id=dev, device_id_type=MESH
        )

    barrier = pltpu.get_barrier_semaphore()

    def greet_z(i, c):
        pl.semaphore_signal(barrier, inc=1, device_id={"space": (z + i) % NZ}, device_id_type=MESH)
        return c

    lax.fori_loop(1, NZ, greet_z, 0)

    def greet_t(i, c):
        pl.semaphore_signal(barrier, inc=1, device_id={"tm": (t + i) % NT}, device_id_type=MESH)
        return c

    lax.fori_loop(1, NT, greet_t, 0)

    def greet_s(i, c):
        pl.semaphore_signal(barrier, inc=1, device_id={"section": nxt, "tm": i}, device_id_type=MESH)
        pl.semaphore_signal(barrier, inc=1, device_id={"section": prv, "tm": i}, device_id_type=MESH)
        return c

    lax.fori_loop(0, NT, greet_s, 0)

    loc_in = [
        pltpu.make_async_copy(a, b, loc.at[3 + i])
        for i, (a, b) in enumerate(((k_hbm, k_ref), (v_hbm, v_ref), (q_hbm, q_ref), (w_hbm, w_ref)))
    ]
    for c in loc_in:
        c.start()
    loc_q = pltpu.make_async_copy(qkv_hbm, wq.at[y], loc.at[0])
    loc_o = pltpu.make_async_copy(ot_hbm, wo.at[y], loc.at[1])
    loc_h = pltpu.make_async_copy(hid_hbm, hid, loc.at[2])
    loc_q.start()
    loc_o.start()
    loc_h.start()

    for c in loc_in:
        c.wait()
    wpad[...] = jnp.concatenate([w_ref[:, 1024:1152].astype(F32), jnp.zeros((8, 128), F32)], axis=0).astype(BF16)
    ws[t, 0, 0, :16] = wpad[pl.ds(pl.multiple_of((t % 5) * 16, 16), 16), :]
    ws[t, 0, 0, 16:] = w_ref[:, pl.ds(pl.multiple_of(t * 128, 128), 128)]
    kt = k_ref[...].astype(F32).T
    vt = v_ref[...].astype(F32).T
    for h in range(NZ):
        kvs[h] = jnp.concatenate([kt[HD * h : HD * (h + 1)], vt[HD * h : HD * (h + 1)]], axis=0).astype(BF16)
    qt = q_ref[...].astype(F32).T
    for h in range(NZ):
        qs[h] = qt[HD * h : HD * (h + 1)].astype(BF16)
    kvr[z] = kvs[z]
    qr[z] = qs[z]

    pl.semaphore_wait(barrier, (NZ - 1) + (NT - 1) + 2 * NT)

    def wz_far(k):
        return remote(ws.at[t, 0, 0], ws.at[t, 0, 4 - k], swz.at[k], rwz.at[k], {"space": (z + 4 * k) % NZ})

    def wz_near(i):
        to, src, dst = (
            ((z + NZ - 1) % NZ, ws.at[t, 0], ws.at[t, 1]),
            ((z + 1) % NZ, ws.at[t, 0], ws.at[t, 3]),
            ((z + NZ - 2) % NZ, ws.at[t, 0, pl.ds(2, 2)], ws.at[t, 2, pl.ds(2, 2)]),
            ((z + 2) % NZ, ws.at[t, 0, pl.ds(1, 2)], ws.at[t, 2, pl.ds(0, 2)]),
        )[i]
        return remote(src, dst, swz.at[4 + i], rwz.at[4 + i], {"space": to})

    for k in (2, 1, 3):
        wz_far(k).start()

    def wq_send(unit, way):
        dev = yr if way == 0 else yl
        if unit < 3:
            return remote(qkv_hbm.at[unit], wq.at[y, unit], sqy.at[way, unit], rqy.at[way, unit], dev)
        return remote(ot_hbm, wo.at[y], sqy.at[way, 3], rqy.at[way, 3], dev)

    for unit in (0, 1, 2, 3):
        wq_send(unit, 0).start()
        wq_send((unit + 2) % 4, 1).start()

    def kv_copy(i):
        to = (z + i) % NZ
        return remote(kvs.at[to], kvr.at[z], skv.at[i], rkv.at[i], {"space": to})

    def q_copy(i):
        to = (z + i) % NZ
        return remote(qs.at[to], qr.at[z], sq.at[i], rq.at[i], {"space": to})

    def kv_start(i):
        kv_copy(NZ - i).start()
        kv_copy(i).start()

    def one(copy):
        copy(8).start()

    def q_start(i):
        q_copy(i).start()
        q_copy(NZ - i).start()

    def take_kv(src):
        block = kvr[src].astype(F32)
        off = pl.ds(pl.multiple_of(src * ROWS, ROWS), ROWS)
        kmat[off, :] = block[:HD].T.astype(BF16)
        vmat[:HD, off] = block[HD:].astype(BF16)

    def kv_take(i, c):
        kv_copy(i).wait_recv()
        take_kv((z + NZ - i) % NZ)
        kv_copy(NZ - i).wait_recv()
        take_kv((z + i) % NZ)
        return c

    def wy_copy(way):
        return remote(ws.at[t], ws.at[t], swy.at[way], rwy.at[way], yr if way == 0 else yl)

    def wy_pass(way):
        dev, tt = (yr, t_yl) if way == 0 else (yl, t_yr)
        part = ws.at[tt, pl.ds(2 * way, 2)]
        return remote(part, part, swy.at[2 + way], rwy.at[2 + way], dev)

    def wx_copy(i):
        part = ws.at[(t, t_yl, t_yr, t_y2)[i]]
        return remote(part, part, swx.at[i], rwx.at[i], xo)

    queue = [(one, kv_copy)] + [(kv_start, i) for i in range(7, 0, -1)] + [(one, q_copy)] + [(q_start, i) for i in range(7, 0, -1)]

    def issue(count):
        for _ in range(count):
            start, what = queue.pop(0)
            start(what)

    issue(PACE[0])
    vmat[HD:, :] = jnp.ones((8, NZ * ROWS), BF16)
    take_kv(z)
    for k in (1, 3, 2):
        wz_far(k).wait_recv()
    for i in range(4):
        wz_near(i).start()
    issue(PACE[1])
    for i in range(4):
        wz_near(i).wait_recv()
    wx_copy(0).start()
    wy_copy(0).start()
    wy_copy(1).start()
    issue(len(queue))

    kv_copy(8).wait_recv()
    take_kv((z + 8) % NZ)
    lax.fori_loop(1, KV1, lambda i, c: kv_take(8 - i, c), 0)
    wy_copy(0).wait_recv()
    wy_pass(0).start()
    wx_copy(1).start()
    wy_copy(1).wait_recv()
    wy_pass(1).start()
    wx_copy(2).start()
    lax.fori_loop(KV1, 8, lambda i, c: kv_take(8 - i, c), 0)

    def wq_pass(unit, way):
        dev, yy = (yr, y_l) if way == 0 else (yl, y_r)
        if unit < 3:
            return remote(wq.at[yy, unit], wq.at[yy, unit], sqy.at[way, 4 + unit], rqy.at[way, 4 + unit], dev)
        return remote(wo.at[yy], wo.at[yy], sqy.at[way, 7], rqy.at[way, 7], dev)

    def o_copy(i):
        to = (z + i) % NZ
        return remote(osd.at[to], orc.at[z], so.at[i], ro.at[i], {"space": to})

    def attend(i, c):
        d = 8 - i
        src_a = (z + NZ - d) % NZ
        src_b = jnp.where(d == 8, z, (z + d) % NZ)
        q_copy(d).wait_recv()

        @pl.when(d < 8)
        def _():
            q_copy(NZ - d).wait_recv()

        queries = jnp.concatenate([qr[src_a], qr[src_b]], axis=1)
        s = jnp.dot(kmat[...], queries, preferred_element_type=F32)
        top = jnp.max(s, axis=0, keepdims=True)
        p = jnp.exp2((s - top) * FACTOR2).astype(BF16)
        o = jnp.dot(vmat[...], p, preferred_element_type=F32)
        o = (o[:HD] / o[HD : HD + 1]).astype(BF16)
        osd[src_a] = o[:, :ROWS]
        osd[src_b] = o[:, ROWS:]
        o_copy(NZ - d).start()

        @pl.when(d < 8)
        def _():
            o_copy(d).start()

        @pl.when(i == 1)
        def _():
            wy_pass(0).wait_recv()
            wy_pass(1).wait_recv()
            wx_copy(3).start()

        @pl.when(i == 4)
        def _():
            for unit, way in ((0, 0), (2, 1), (1, 0), (3, 1)):
                wq_send(unit, way).wait_recv()
                wq_pass(unit, way).start()

        return c

    lax.fori_loop(0, 8, attend, 0)
    orc[z] = osd[z]

    for i in range(4):
        wx_copy(i).wait_recv()

    def w_rows(i, c):
        m, k = i // 4, i % 4
        for b in range(8):
            wall[i, :, 128 * b : 128 * (b + 1)] = ws[b, m, k, 16:]
        last = [ws[b, m, k, :16].astype(F32) for b in range(5)]
        wall[i, :, 1024:] = jnp.concatenate(last, axis=0)[:HD].astype(BF16)
        return c

    lax.fori_loop(0, NZ, w_rows, 0)

    def project(r):
        slot = (r % 4) * 4 + ((r + 1) // 4) % 4
        return jnp.dot(orc[(z + r) % NZ].astype(F32).T.astype(BF16), wall[slot], preferred_element_type=F32)

    def o_take(i, c):
        d = 8 - i
        o_copy(d).wait_recv()
        o_copy(NZ - d).wait_recv()
        acc[...] += project(NZ - d) + project(d)
        return c

    acc[...] = project(0)
    o_copy(8).wait_recv()
    acc[...] += project(8)
    lax.fori_loop(1, 7, o_take, 0)
    o_copy(1).wait_recv()
    o_copy(NZ - 1).wait_recv()
    loc_h.wait()
    projected = acc[...] + project(NZ - 1) + project(1)
    mids[...] = (hid[...].astype(F32) + gs_ref[...] * projected).astype(BF16)

    def mid_copy(i, part):
        to = (t + i) % NT
        rows = pl.ds(pl.multiple_of((to // 2) * PART + HALF * part, HALF), HALF)
        return remote(mids.at[rows], midr.at[part, t], sm.at[part, i], rm.at[part, i], {"tm": to})

    for part in range(2):
        for i in (5, 3, 1, 7, 4, 2, 6):
            mid_copy(i, part).start()
        midr[part, t] = mids[pl.ds(pl.multiple_of(y * PART + HALF * part, HALF), HALF), :]

    loc_q.wait()
    loc_o.wait()
    for unit, way in ((2, 0), (3, 0), (0, 1), (1, 1)):
        wq_send(unit, way).wait_recv()
    for unit, way in ((0, 0), (2, 1), (1, 0), (3, 1)):
        wq_pass(unit, way).wait_recv()

    tokens = NT * HALF
    same = (lax.broadcasted_iota(jnp.int32, (tokens, tokens), 0) % HALF) == (
        lax.broadcasted_iota(jnp.int32, (tokens, tokens), 1) % HALF
    )
    keep = jnp.where(xh == 0, 1.0, 0.0).astype(F32)
    ones = jnp.ones((8, tokens), F32)

    def fin_copy(f, part):
        return remote(
            fins.at[part, f], finr.at[t, pl.ds(HALF * part, HALF)], sf.at[part, f], rf.at[part, t],
            {"section": nxt, "tm": f},
        )

    for part in range(2):
        for i in range(1, NT):
            mid_copy(i, part).wait_recv()
        middle = midr[part].reshape(tokens, D).astype(F32)
        centred = middle - jnp.mean(middle, axis=-1, keepdims=True)
        variance = jnp.mean(centred * centred, axis=-1, keepdims=True)
        normed = (centred * lax.rsqrt(variance + 1e-06) * (1.0 + sc_ref[...]) + sh_ref[...]).astype(BF16)
        proj[...] = lax.dot_general(
            normed, wq[...].reshape(12 * 144, D), (((1,), (1,)), ((), ())), preferred_element_type=F32
        ).T
        for head in range(8):
            at = 432 * (head // 2) + HD * (head % 2)
            tq = proj[at : at + HD, :].astype(BF16)
            tk = proj[at + 144 : at + 144 + HD].T.astype(BF16)
            tv = jnp.concatenate([proj[at + 288 : at + 288 + HD], ones], axis=0).astype(BF16)
            s = jnp.where(same, jnp.dot(tk, tq, preferred_element_type=F32), -jnp.inf)
            p = jnp.exp2((s - jnp.max(s, axis=0, keepdims=True)) * FACTOR2).astype(BF16)
            o = jnp.dot(tv, p, preferred_element_type=F32)
            mixt[HD * head : HD * (head + 1), :] = o[:HD] / o[HD : HD + 1]
        mixed = mixt[...].T.astype(BF16)
        summed = jnp.dot(mixed, wo[...].reshape(576, D), preferred_element_type=F32)
        done = keep * middle + gt_ref[...] * summed
        fins[part] = done.astype(BF16).reshape(NT, HALF, D)
        for f in range(NT):
            fin_copy(f, part).start()

    def fin_wait(f, c):
        for part in range(2):
            remote(
                fins.at[part, f], finr.at[f, pl.ds(HALF * part, HALF)], sf.at[part, f], rf.at[part, f],
                {"section": nxt, "tm": f},
            ).wait_recv()
        return c

    lax.fori_loop(0, NT, fin_wait, 0)

    def left_z(i, c):
        kv_copy(i).wait_send()
        q_copy(i).wait_send()
        o_copy(i).wait_send()
        return c

    lax.fori_loop(1, NZ, left_z, 0)

    for k in range(1, 4):
        wz_far(k).wait_send()
    for i in range(4):
        wz_near(i).wait_send()
        wy_copy(i).wait_send() if i < 2 else wy_pass(i - 2).wait_send()
        wx_copy(i).wait_send()
        for way in range(2):
            wq_send(i, way).wait_send()
    for unit, way in ((0, 0), (2, 1), (1, 0), (3, 1)):
        wq_pass(unit, way).wait_send()

    def left_t(i, c):
        mid_copy(i, 0).wait_send()
        mid_copy(i, 1).wait_send()
        return c

    lax.fori_loop(1, NT, left_t, 0)

    def left_f(f, c):
        fin_copy(f, 0).wait_send()
        fin_copy(f, 1).wait_send()
        return c

    lax.fori_loop(0, NT, left_f, 0)


def shards(
    hidden_in, query_s, key_s, value_s, out_proj_s, gate_s, shift_t, scale_t, qkv_t, out_t, gate_t
):
    vm = pl.BlockSpec(memory_space=pltpu.VMEM)
    hbm = pl.BlockSpec(memory_space=pl.ANY)
    dma = pltpu.SemaphoreType.DMA
    plane = (HD, ROWS)
    out = pl.pallas_call(
        kernel,
        out_shape=jax.ShapeDtypeStruct((NT, PART, D), BF16),
        in_specs=[hbm, hbm, hbm, hbm, hbm, vm, vm, vm, hbm, hbm, vm],
        out_specs=hbm,
        scratch_shapes=[
            pltpu.VMEM((ROWS, D), BF16),
            pltpu.VMEM((ROWS, D), BF16),
            pltpu.VMEM((ROWS, D), BF16),
            pltpu.VMEM((HD, D), BF16),
            pltpu.VMEM((NZ, 2 * HD, ROWS), BF16),
            pltpu.VMEM((NZ, 2 * HD, ROWS), BF16),
            pltpu.VMEM((NZ, *plane), BF16),
            pltpu.VMEM((NZ, *plane), BF16),
            pltpu.VMEM((NZ, *plane), BF16),
            pltpu.VMEM((NZ, *plane), BF16),
            pltpu.VMEM((80, 128), BF16),
            pltpu.VMEM((NT, 4, 4, 88, 128), BF16),
            pltpu.VMEM((NZ, HD, D), BF16),
            pltpu.VMEM((ROWS, D), F32),
            pltpu.VMEM((NZ * ROWS, HD), BF16),
            pltpu.VMEM((HD + 8, NZ * ROWS), BF16),
            pltpu.VMEM((4, 3, 144, D), BF16),
            pltpu.VMEM((4, 144, D), BF16),
            pltpu.VMEM((ROWS, D), BF16),
            pltpu.VMEM((ROWS, D), BF16),
            pltpu.VMEM((2, NT, HALF, D), BF16),
            pltpu.VMEM((1728, NT * HALF), F32),
            pltpu.VMEM((576, NT * HALF), F32),
            pltpu.VMEM((2, NT, HALF, D), BF16),
            dma((NZ,)), dma((NZ,)), dma((NZ,)), dma((NZ,)), dma((NZ,)), dma((NZ,)),
            dma((8,)), dma((8,)), dma((4,)), dma((4,)), dma((4,)), dma((4,)),
            dma((2, 8)), dma((2, 8)), dma((2, NT)), dma((2, NT)), dma((2, NT)), dma((2, NT)), dma((7,)),
        ],
        compiler_params=pltpu.CompilerParams(
            collective_id=0, has_side_effects=True, vmem_limit_bytes=56 * 1024 * 1024
        ),
        cost_estimate=pl.CostEstimate(flops=3_000_000_000, bytes_accessed=6_000_000, transcendentals=4_500_000),
        name="st_block_pair",
    )(
        query_s[0, 0], key_s[0, 0], value_s[0, 0], hidden_in[0, 0], out_proj_s[0],
        gate_s, shift_t, scale_t, qkv_t[0], out_t[0], gate_t,
    )
    halves = out.reshape(4, 2, PART, D)
    return (halves[:, 0] + halves[:, 1]).reshape(1, 1, ROWS, D)


def solution(mesh):
    in_specs = (
        P("section", "tm", "space", None),
        P("section", "tm", "space", None),
        P("section", "tm", "space", None),
        P("section", "tm", "space", None),
        P("section", "space", None),
        P("section", None),
        P("section", None),
        P("section", None),
        P("section", None, "tm", None),
        P("section", "tm", None),
        P("section", None),
    )
    out_specs = P("section", "tm", "space", None)
    return jax.shard_map(shards, mesh=mesh, in_specs=in_specs, out_specs=out_specs, check_vma=False)
```

```python
import jax
import jax.numpy as jnp
from jax import lax
from jax.experimental import pallas as pl
from jax.experimental.pallas import tpu as pltpu
from jax.sharding import PartitionSpec as P

MESH = pl.DeviceIdType.MESH
F32 = jnp.float32
BF16 = jnp.bfloat16
D = 1152
HD = 72
NZ = 16
NT = 8
NS = 4
ROWS = 128
PART = 32
HALF = 16
PACE = (2, 1, 1, 1)
KV1 = 5
FACTOR = HD ** (-0.5)
FACTOR2 = FACTOR * 1.4426950408889634


def kernel(
    q_hbm, k_hbm, v_hbm, hid_hbm, w_hbm, gs_ref, sh_ref, sc_ref, qkv_hbm, ot_hbm, gt_ref,
    finr,
    q_ref, k_ref, v_ref, w_ref, kvs, kvr, qs, qr, osd, orc, wpad, ws, wall, acc, kmat, vmat, wq, wo, hid, mids, midr, proj, mixt, fins,
    skv, rkv, sq, rq, so, ro, swz, rwz, swy, rwy, swx, rwx, sqy, rqy, sm, rm, sf, rf, loc,
):
    sec = lax.axis_index("section")
    t = lax.axis_index("tm")
    z = lax.axis_index("space")
    y = t // 2
    xh = t % 2
    nxt = (sec + 1) % NS
    prv = (sec + NS - 1) % NS
    zr = {"space": (z + 1) % NZ}
    zl = {"space": (z + NZ - 1) % NZ}
    yr = {"tm": (t + 2) % NT}
    yl = {"tm": (t + NT - 2) % NT}
    xo = {"tm": t + 1 - 2 * xh}
    t_yr = (t + 2) % NT
    t_yl = (t + NT - 2) % NT
    t_y2 = (t + 4) % NT
    y_r = (y + 1) % 4
    y_l = (y + 3) % 4

    def remote(src, dst, s_sem, r_sem, dev):
        return pltpu.make_async_remote_copy(
            src_ref=src, dst_ref=dst, send_sem=s_sem, recv_sem=r_sem, device_id=dev, device_id_type=MESH
        )

    barrier = pltpu.get_barrier_semaphore()

    def greet_z(i, c):
        pl.semaphore_signal(barrier, inc=1, device_id={"space": (z + i) % NZ}, device_id_type=MESH)
        return c

    greet_z(8, 0)
    lax.fori_loop(1, 8, lambda i, c: greet_z(8 + i, greet_z(8 - i, c)), 0)

    loc_in = [
        pltpu.make_async_copy(a, b, loc.at[3 + i])
        for i, (a, b) in enumerate(((k_hbm, k_ref), (v_hbm, v_ref), (q_hbm, q_ref), (w_hbm, w_ref)))
    ]
    for c in loc_in:
        c.start()
    def greet_t(i, c):
        pl.semaphore_signal(barrier, inc=1, device_id={"tm": (t + i) % NT}, device_id_type=MESH)
        return c

    lax.fori_loop(1, NT, greet_t, 0)

    def greet_s(i, c):
        pl.semaphore_signal(barrier, inc=1, device_id={"section": nxt, "tm": i}, device_id_type=MESH)
        pl.semaphore_signal(barrier, inc=1, device_id={"section": prv, "tm": i}, device_id_type=MESH)
        return c

    lax.fori_loop(0, NT, greet_s, 0)

    loc_q = pltpu.make_async_copy(qkv_hbm, wq.at[y], loc.at[0])
    loc_o = pltpu.make_async_copy(ot_hbm, wo.at[y], loc.at[1])
    loc_h = pltpu.make_async_copy(hid_hbm, hid, loc.at[2])
    loc_q.start()
    loc_o.start()
    loc_h.start()

    for c in loc_in:
        c.wait()
    wpad[...] = jnp.concatenate([w_ref[:, 1024:1152].astype(F32), jnp.zeros((8, 128), F32)], axis=0).astype(BF16)
    ws[t, 0, 0, :16] = wpad[pl.ds(pl.multiple_of((t % 5) * 16, 16), 16), :]
    ws[t, 0, 0, 16:] = w_ref[:, pl.ds(pl.multiple_of(t * 128, 128), 128)]
    kt = k_ref[...].astype(F32).T
    vt = v_ref[...].astype(F32).T
    for h in range(NZ):
        kvs[h] = jnp.concatenate([kt[HD * h : HD * (h + 1)], vt[HD * h : HD * (h + 1)]], axis=0).astype(BF16)
    qt = q_ref[...].astype(F32).T
    for h in range(NZ):
        qs[h] = qt[HD * h : HD * (h + 1)].astype(BF16)
    kvr[z] = kvs[z]
    qr[z] = qs[z]

    pl.semaphore_wait(barrier, (NZ - 1) + (NT - 1) + 2 * NT)

    def wz_far(k):
        return remote(ws.at[t, 0, 0], ws.at[t, 0, 4 - k], swz.at[k], rwz.at[k], {"space": (z + 4 * k) % NZ})

    def wz_opposite():
        return remote(ws.at[t, 0, 3], ws.at[t, 0, 2], swz.at[2], rwz.at[2], {"space": (z + 4) % NZ})

    def wz_near(i):
        dev, src, dst = (
            (zl, ws.at[t, 0], ws.at[t, 1]),
            (zr, ws.at[t, 0], ws.at[t, 3]),
            (zl, ws.at[t, 1, pl.ds(2, 2)], ws.at[t, 2, pl.ds(2, 2)]),
            (zr, ws.at[t, 3, pl.ds(1, 2)], ws.at[t, 2, pl.ds(0, 2)]),
        )[i]
        return remote(src, dst, swz.at[4 + i], rwz.at[4 + i], dev)

    for k in (1, 3):
        wz_far(k).start()

    def wq_send(unit, way):
        dev = yr if way == 0 else yl
        if unit < 3:
            return remote(qkv_hbm.at[unit], wq.at[y, unit], sqy.at[way, unit], rqy.at[way, unit], dev)
        return remote(ot_hbm, wo.at[y], sqy.at[way, 3], rqy.at[way, 3], dev)

    for unit in (0, 1, 2, 3):
        wq_send(unit, 0).start()
        wq_send((unit + 2) % 4, 1).start()

    def kv_copy(i):
        to = (z + i) % NZ
        return remote(kvs.at[to], kvr.at[z], skv.at[i], rkv.at[i], {"space": to})

    def q_copy(i):
        to = (z + i) % NZ
        return remote(qs.at[to], qr.at[z], sq.at[i], rq.at[i], {"space": to})

    def kv_start(i):
        kv_copy(NZ - i).start()
        kv_copy(i).start()

    def one(copy):
        copy(8).start()

    def q_start(i):
        q_copy(i).start()
        q_copy(NZ - i).start()

    def take_kv(src):
        block = kvr[src].astype(F32)
        off = pl.ds(pl.multiple_of(src * ROWS, ROWS), ROWS)
        kmat[off, :] = block[:HD].T.astype(BF16)
        vmat[:HD, off] = block[HD:].astype(BF16)

    def kv_take(i, c):
        kv_copy(i).wait_recv()
        take_kv((z + NZ - i) % NZ)
        kv_copy(NZ - i).wait_recv()
        take_kv((z + i) % NZ)
        return c

    def wy_copy(way):
        return remote(ws.at[t], ws.at[t], swy.at[way], rwy.at[way], yr if way == 0 else yl)

    def wy_pass(way):
        dev, tt = (yr, t_yl) if way == 0 else (yl, t_yr)
        part = ws.at[tt, pl.ds(2 * way, 2)]
        return remote(part, part, swy.at[2 + way], rwy.at[2 + way], dev)

    def wx_copy(i):
        part = ws.at[(t, t_yl, t_yr, t_y2)[i]]
        return remote(part, part, swx.at[i], rwx.at[i], xo)

    queue = [(one, kv_copy)] + [(kv_start, i) for i in range(7, 0, -1)] + [(one, q_copy)] + [(q_start, i) for i in range(7, 0, -1)]

    def issue(count):
        for _ in range(count):
            start, what = queue.pop(0)
            start(what)

    issue(PACE[0])
    vmat[HD:, :] = jnp.ones((8, NZ * ROWS), BF16)
    take_kv(z)
    wz_far(1).wait_recv()
    wz_opposite().start()
    wz_far(3).wait_recv()
    issue(PACE[1])
    wz_opposite().wait_recv()
    wz_near(0).start()
    wz_near(1).start()
    issue(PACE[2])
    wz_near(0).wait_recv()
    wz_near(2).start()
    wz_near(1).wait_recv()
    wz_near(3).start()
    issue(PACE[3])
    wz_near(2).wait_recv()
    wz_near(3).wait_recv()
    wx_copy(0).start()
    wy_copy(0).start()
    wy_copy(1).start()
    issue(len(queue))

    kv_copy(8).wait_recv()
    take_kv((z + 8) % NZ)
    lax.fori_loop(1, KV1, lambda i, c: kv_take(8 - i, c), 0)
    wy_copy(0).wait_recv()
    wy_pass(0).start()
    wx_copy(1).start()
    wy_copy(1).wait_recv()
    wy_pass(1).start()
    wx_copy(2).start()
    lax.fori_loop(KV1, 8, lambda i, c: kv_take(8 - i, c), 0)

    def wq_pass(unit, way):
        dev, yy = (yr, y_l) if way == 0 else (yl, y_r)
        if unit < 3:
            return remote(wq.at[yy, unit], wq.at[yy, unit], sqy.at[way, 4 + unit], rqy.at[way, 4 + unit], dev)
        return remote(wo.at[yy], wo.at[yy], sqy.at[way, 7], rqy.at[way, 7], dev)

    def o_copy(i):
        to = (z + i) % NZ
        return remote(osd.at[to], orc.at[z], so.at[i], ro.at[i], {"space": to})

    def attend(i, c):
        d = 8 - i
        src_a = (z + NZ - d) % NZ
        src_b = jnp.where(d == 8, z, (z + d) % NZ)
        q_copy(d).wait_recv()

        @pl.when(d < 8)
        def _():
            q_copy(NZ - d).wait_recv()

        queries = jnp.concatenate([qr[src_a], qr[src_b]], axis=1)
        s = jnp.dot(kmat[...], queries, preferred_element_type=F32)
        top = jnp.max(s, axis=0, keepdims=True)
        p = jnp.exp2((s - top) * FACTOR2).astype(BF16)
        o = jnp.dot(vmat[...], p, preferred_element_type=F32)
        o = (o[:HD] / o[HD : HD + 1]).astype(BF16)
        osd[src_a] = o[:, :ROWS]
        osd[src_b] = o[:, ROWS:]
        o_copy(NZ - d).start()

        @pl.when(d < 8)
        def _():
            o_copy(d).start()

        @pl.when(i == 1)
        def _():
            wy_pass(0).wait_recv()
            wy_pass(1).wait_recv()
            wx_copy(3).start()

        @pl.when(i == 4)
        def _():
            for unit, way in ((0, 0), (2, 1), (1, 0), (3, 1)):
                wq_send(unit, way).wait_recv()
                wq_pass(unit, way).start()

        return c

    lax.fori_loop(0, 8, attend, 0)
    orc[z] = osd[z]

    for i in range(4):
        wx_copy(i).wait_recv()

    def w_rows(i, c):
        m, k = i // 4, i % 4
        for b in range(8):
            wall[i, :, 128 * b : 128 * (b + 1)] = ws[b, m, k, 16:]
        last = [ws[b, m, k, :16].astype(F32) for b in range(5)]
        wall[i, :, 1024:] = jnp.concatenate(last, axis=0)[:HD].astype(BF16)
        return c

    lax.fori_loop(0, NZ, w_rows, 0)

    def project(r):
        slot = (r % 4) * 4 + ((r + 1) // 4) % 4
        return jnp.dot(orc[(z + r) % NZ].astype(F32).T.astype(BF16), wall[slot], preferred_element_type=F32)

    def o_take(i, c):
        d = 8 - i
        o_copy(d).wait_recv()
        o_copy(NZ - d).wait_recv()
        acc[...] += project(NZ - d) + project(d)
        return c

    acc[...] = project(0)
    o_copy(8).wait_recv()
    acc[...] += project(8)
    lax.fori_loop(1, 7, o_take, 0)
    o_copy(1).wait_recv()
    o_copy(NZ - 1).wait_recv()
    loc_h.wait()
    projected = acc[...] + project(NZ - 1) + project(1)
    mids[...] = (hid[...].astype(F32) + gs_ref[...] * projected).astype(BF16)

    def mid_copy(i, part):
        to = (t + i) % NT
        rows = pl.ds(pl.multiple_of((to // 2) * PART + HALF * part, HALF), HALF)
        return remote(mids.at[rows], midr.at[part, t], sm.at[part, i], rm.at[part, i], {"tm": to})

    for part in range(2):
        for i in (5, 3, 1, 7, 4, 2, 6):
            mid_copy(i, part).start()
        midr[part, t] = mids[pl.ds(pl.multiple_of(y * PART + HALF * part, HALF), HALF), :]

    loc_q.wait()
    loc_o.wait()
    for unit, way in ((2, 0), (3, 0), (0, 1), (1, 1)):
        wq_send(unit, way).wait_recv()
    for unit, way in ((0, 0), (2, 1), (1, 0), (3, 1)):
        wq_pass(unit, way).wait_recv()

    tokens = NT * HALF
    same = (lax.broadcasted_iota(jnp.int32, (tokens, tokens), 0) % HALF) == (
        lax.broadcasted_iota(jnp.int32, (tokens, tokens), 1) % HALF
    )
    keep = jnp.where(xh == 0, 1.0, 0.0).astype(F32)
    ones = jnp.ones((8, tokens), F32)

    def fin_copy(f, part):
        return remote(
            fins.at[part, f], finr.at[t, pl.ds(HALF * part, HALF)], sf.at[part, f], rf.at[part, t],
            {"section": nxt, "tm": f},
        )

    for part in range(2):
        for i in range(1, NT):
            mid_copy(i, part).wait_recv()
        middle = midr[part].reshape(tokens, D).astype(F32)
        centred = middle - jnp.mean(middle, axis=-1, keepdims=True)
        variance = jnp.mean(centred * centred, axis=-1, keepdims=True)
        normed = (centred * lax.rsqrt(variance + 1e-06) * (1.0 + sc_ref[...]) + sh_ref[...]).astype(BF16)
        proj[...] = lax.dot_general(
            normed, wq[...].reshape(12 * 144, D), (((1,), (1,)), ((), ())), preferred_element_type=F32
        ).T
        for head in range(8):
            at = 432 * (head // 2) + HD * (head % 2)
            tq = proj[at : at + HD, :].astype(BF16)
            tk = proj[at + 144 : at + 144 + HD].T.astype(BF16)
            tv = jnp.concatenate([proj[at + 288 : at + 288 + HD], ones], axis=0).astype(BF16)
            s = jnp.where(same, jnp.dot(tk, tq, preferred_element_type=F32), -jnp.inf)
            p = jnp.exp2((s - jnp.max(s, axis=0, keepdims=True)) * FACTOR2).astype(BF16)
            o = jnp.dot(tv, p, preferred_element_type=F32)
            mixt[HD * head : HD * (head + 1), :] = o[:HD] / o[HD : HD + 1]
        mixed = mixt[...].T.astype(BF16)
        summed = jnp.dot(mixed, wo[...].reshape(576, D), preferred_element_type=F32)
        done = keep * middle + gt_ref[...] * summed
        fins[part] = done.astype(BF16).reshape(NT, HALF, D)
        for f in range(NT):
            fin_copy(f, part).start()

    def fin_wait(f, c):
        for part in range(2):
            remote(
                fins.at[part, f], finr.at[f, pl.ds(HALF * part, HALF)], sf.at[part, f], rf.at[part, f],
                {"section": nxt, "tm": f},
            ).wait_recv()
        return c

    lax.fori_loop(0, NT, fin_wait, 0)

    def left_z(i, c):
        kv_copy(i).wait_send()
        q_copy(i).wait_send()
        o_copy(i).wait_send()
        return c

    lax.fori_loop(1, NZ, left_z, 0)

    wz_far(1).wait_send()
    wz_far(3).wait_send()
    wz_opposite().wait_send()
    for i in range(4):
        wz_near(i).wait_send()
        wy_copy(i).wait_send() if i < 2 else wy_pass(i - 2).wait_send()
        wx_copy(i).wait_send()
        for way in range(2):
            wq_send(i, way).wait_send()
    for unit, way in ((0, 0), (2, 1), (1, 0), (3, 1)):
        wq_pass(unit, way).wait_send()

    def left_t(i, c):
        mid_copy(i, 0).wait_send()
        mid_copy(i, 1).wait_send()
        return c

    lax.fori_loop(1, NT, left_t, 0)

    def left_f(f, c):
        fin_copy(f, 0).wait_send()
        fin_copy(f, 1).wait_send()
        return c

    lax.fori_loop(0, NT, left_f, 0)


def shards(
    hidden_in, query_s, key_s, value_s, out_proj_s, gate_s, shift_t, scale_t, qkv_t, out_t, gate_t
):
    vm = pl.BlockSpec(memory_space=pltpu.VMEM)
    hbm = pl.BlockSpec(memory_space=pl.ANY)
    dma = pltpu.SemaphoreType.DMA
    plane = (HD, ROWS)
    out = pl.pallas_call(
        kernel,
        out_shape=jax.ShapeDtypeStruct((NT, PART, D), BF16),
        in_specs=[hbm, hbm, hbm, hbm, hbm, vm, vm, vm, hbm, hbm, vm],
        out_specs=hbm,
        scratch_shapes=[
            pltpu.VMEM((ROWS, D), BF16),
            pltpu.VMEM((ROWS, D), BF16),
            pltpu.VMEM((ROWS, D), BF16),
            pltpu.VMEM((HD, D), BF16),
            pltpu.VMEM((NZ, 2 * HD, ROWS), BF16),
            pltpu.VMEM((NZ, 2 * HD, ROWS), BF16),
            pltpu.VMEM((NZ, *plane), BF16),
            pltpu.VMEM((NZ, *plane), BF16),
            pltpu.VMEM((NZ, *plane), BF16),
            pltpu.VMEM((NZ, *plane), BF16),
            pltpu.VMEM((80, 128), BF16),
            pltpu.VMEM((NT, 4, 4, 88, 128), BF16),
            pltpu.VMEM((NZ, HD, D), BF16),
            pltpu.VMEM((ROWS, D), F32),
            pltpu.VMEM((NZ * ROWS, HD), BF16),
            pltpu.VMEM((HD + 8, NZ * ROWS), BF16),
            pltpu.VMEM((4, 3, 144, D), BF16),
            pltpu.VMEM((4, 144, D), BF16),
            pltpu.VMEM((ROWS, D), BF16),
            pltpu.VMEM((ROWS, D), BF16),
            pltpu.VMEM((2, NT, HALF, D), BF16),
            pltpu.VMEM((1728, NT * HALF), F32),
            pltpu.VMEM((576, NT * HALF), F32),
            pltpu.VMEM((2, NT, HALF, D), BF16),
            dma((NZ,)), dma((NZ,)), dma((NZ,)), dma((NZ,)), dma((NZ,)), dma((NZ,)),
            dma((8,)), dma((8,)), dma((4,)), dma((4,)), dma((4,)), dma((4,)),
            dma((2, 8)), dma((2, 8)), dma((2, NT)), dma((2, NT)), dma((2, NT)), dma((2, NT)), dma((7,)),
        ],
        compiler_params=pltpu.CompilerParams(
            collective_id=0, has_side_effects=True, vmem_limit_bytes=56 * 1024 * 1024
        ),
        cost_estimate=pl.CostEstimate(flops=3_000_000_000, bytes_accessed=6_000_000, transcendentals=4_500_000),
        name="st_block_pair",
    )(
        query_s[0, 0], key_s[0, 0], value_s[0, 0], hidden_in[0, 0], out_proj_s[0],
        gate_s, shift_t, scale_t, qkv_t[0], out_t[0], gate_t,
    )
    halves = out.reshape(4, 2, PART, D)
    return (halves[:, 0] + halves[:, 1]).reshape(1, 1, ROWS, D)


def solution(mesh):
    in_specs = (
        P("section", "tm", "space", None),
        P("section", "tm", "space", None),
        P("section", "tm", "space", None),
        P("section", "tm", "space", None),
        P("section", "space", None),
        P("section", None),
        P("section", None),
        P("section", None),
        P("section", None, "tm", None),
        P("section", "tm", None),
        P("section", None),
    )
    out_specs = P("section", "tm", "space", None)
    return jax.shard_map(shards, mesh=mesh, in_specs=in_specs, out_specs=out_specs, check_vma=False)
```

```python
import jax
import jax.numpy as jnp
from jax import lax
from jax.experimental import pallas as pl
from jax.experimental.pallas import tpu as pltpu
from jax.sharding import PartitionSpec as P

MESH = pl.DeviceIdType.MESH
F32 = jnp.float32
BF16 = jnp.bfloat16
D = 1152
HD = 72
NZ = 16
NT = 8
NS = 4
ROWS = 128
PART = 32
HALF = 16
PACE = (2, 1, 1, 1)
KV1 = 5
FACTOR = HD ** (-0.5)
FACTOR2 = FACTOR * 1.4426950408889634


def kernel(
    q_hbm, k_hbm, v_hbm, hid_hbm, w_hbm, gs_ref, sh_ref, sc_ref, qkv_hbm, ot_hbm, gt_ref,
    finr,
    q_ref, k_ref, v_ref, w_ref, kvs, kvr, qs, qr, osd, orc, wpad, ws, wall, acc, kmat, vmat, wq, wo, hid, mids, midr, proj, mixt, fins,
    skv, rkv, sq, rq, so, ro, swz, rwz, swy, rwy, swx, rwx, sqy, rqy, sm, rm, sf, rf, loc,
):
    sec = lax.axis_index("section")
    t = lax.axis_index("tm")
    z = lax.axis_index("space")
    y = t // 2
    xh = t % 2
    nxt = (sec + 1) % NS
    prv = (sec + NS - 1) % NS
    zr = {"space": (z + 1) % NZ}
    zl = {"space": (z + NZ - 1) % NZ}
    yr = {"tm": (t + 2) % NT}
    yl = {"tm": (t + NT - 2) % NT}
    xo = {"tm": t + 1 - 2 * xh}
    t_yr = (t + 2) % NT
    t_yl = (t + NT - 2) % NT
    t_y2 = (t + 4) % NT
    y_r = (y + 1) % 4
    y_l = (y + 3) % 4

    def remote(src, dst, s_sem, r_sem, dev):
        return pltpu.make_async_remote_copy(
            src_ref=src, dst_ref=dst, send_sem=s_sem, recv_sem=r_sem, device_id=dev, device_id_type=MESH
        )

    barrier = pltpu.get_barrier_semaphore()

    def greet_z(i, c):
        pl.semaphore_signal(barrier, inc=1, device_id={"space": (z + i) % NZ}, device_id_type=MESH)
        return c

    greet_z(8, 0)
    lax.fori_loop(1, 8, lambda i, c: greet_z(8 + i, greet_z(8 - i, c)), 0)

    loc_in = [
        pltpu.make_async_copy(a, b, loc.at[3 + i])
        for i, (a, b) in enumerate(((k_hbm, k_ref), (v_hbm, v_ref), (q_hbm, q_ref), (w_hbm, w_ref)))
    ]
    for c in loc_in:
        c.start()
    def greet_t(i, c):
        pl.semaphore_signal(barrier, inc=1, device_id={"tm": (t + i) % NT}, device_id_type=MESH)
        return c

    lax.fori_loop(1, NT, greet_t, 0)

    def greet_s(i, c):
        pl.semaphore_signal(barrier, inc=1, device_id={"section": nxt, "tm": i}, device_id_type=MESH)
        pl.semaphore_signal(barrier, inc=1, device_id={"section": prv, "tm": i}, device_id_type=MESH)
        return c

    lax.fori_loop(0, NT, greet_s, 0)

    loc_q = pltpu.make_async_copy(qkv_hbm, wq.at[y], loc.at[0])
    loc_o = pltpu.make_async_copy(ot_hbm, wo.at[y], loc.at[1])
    loc_h = pltpu.make_async_copy(hid_hbm, hid, loc.at[2])
    loc_q.start()
    loc_o.start()
    loc_h.start()

    for c in loc_in:
        c.wait()
    wpad[...] = jnp.concatenate([w_ref[:, 1024:1152].astype(F32), jnp.zeros((8, 128), F32)], axis=0).astype(BF16)
    ws[t, 0, 0, :16] = wpad[pl.ds(pl.multiple_of((t % 5) * 16, 16), 16), :]
    ws[t, 0, 0, 16:] = w_ref[:, pl.ds(pl.multiple_of(t * 128, 128), 128)]
    kt = k_ref[...].astype(F32).T
    vt = v_ref[...].astype(F32).T
    for h in range(NZ):
        kvs[h] = jnp.concatenate([kt[HD * h : HD * (h + 1)], vt[HD * h : HD * (h + 1)]], axis=0).astype(BF16)
    kvr[z] = kvs[z]

    pl.semaphore_wait(barrier, (NZ - 1) + (NT - 1) + 2 * NT)

    def wz_far(k):
        return remote(ws.at[t, 0, 0], ws.at[t, 0, 4 - k], swz.at[k], rwz.at[k], {"space": (z + 4 * k) % NZ})

    def wz_opposite():
        return remote(ws.at[t, 0, 3], ws.at[t, 0, 2], swz.at[2], rwz.at[2], {"space": (z + 4) % NZ})

    def wz_near(i):
        dev, src, dst = (
            (zl, ws.at[t, 0], ws.at[t, 1]),
            (zr, ws.at[t, 0], ws.at[t, 3]),
            (zl, ws.at[t, 1, pl.ds(2, 2)], ws.at[t, 2, pl.ds(2, 2)]),
            (zr, ws.at[t, 3, pl.ds(1, 2)], ws.at[t, 2, pl.ds(0, 2)]),
        )[i]
        return remote(src, dst, swz.at[4 + i], rwz.at[4 + i], dev)

    for k in (1, 3):
        wz_far(k).start()

    def wq_send(unit, way):
        dev = yr if way == 0 else yl
        if unit < 3:
            return remote(qkv_hbm.at[unit], wq.at[y, unit], sqy.at[way, unit], rqy.at[way, unit], dev)
        return remote(ot_hbm, wo.at[y], sqy.at[way, 3], rqy.at[way, 3], dev)

    for unit in (0, 1, 2, 3):
        wq_send(unit, 0).start()
        wq_send((unit + 2) % 4, 1).start()

    def kv_copy(i):
        to = (z + i) % NZ
        return remote(kvs.at[to], kvr.at[z], skv.at[i], rkv.at[i], {"space": to})

    def q_copy(i):
        to = (z + i) % NZ
        return remote(qs.at[to], qr.at[z], sq.at[i], rq.at[i], {"space": to})

    def kv_start(i):
        kv_copy(NZ - i).start()
        kv_copy(i).start()

    def one(copy):
        copy(8).start()

    def q_start(i):
        q_copy(i).start()
        q_copy(NZ - i).start()

    def take_kv(src):
        block = kvr[src].astype(F32)
        off = pl.ds(pl.multiple_of(src * ROWS, ROWS), ROWS)
        kmat[off, :] = block[:HD].T.astype(BF16)
        vmat[:HD, off] = block[HD:].astype(BF16)

    def kv_take(i, c):
        kv_copy(i).wait_recv()
        take_kv((z + NZ - i) % NZ)
        kv_copy(NZ - i).wait_recv()
        take_kv((z + i) % NZ)
        return c

    def wy_copy(way):
        return remote(ws.at[t], ws.at[t], swy.at[way], rwy.at[way], yr if way == 0 else yl)

    def wy_pass(way):
        dev, tt = (yr, t_yl) if way == 0 else (yl, t_yr)
        part = ws.at[tt, pl.ds(2 * way, 2)]
        return remote(part, part, swy.at[2 + way], rwy.at[2 + way], dev)

    def wx_copy(i):
        part = ws.at[(t, t_yl, t_yr, t_y2)[i]]
        return remote(part, part, swx.at[i], rwx.at[i], xo)

    queue = [(one, kv_copy)] + [(kv_start, i) for i in range(7, 0, -1)] + [(one, q_copy)] + [(q_start, i) for i in range(7, 0, -1)]

    def issue(count):
        for _ in range(count):
            start, what = queue.pop(0)
            start(what)

    issue(PACE[0])
    qt = q_ref[...].astype(F32).T
    for h in range(NZ):
        qs[h] = qt[HD * h : HD * (h + 1)].astype(BF16)
    qr[z] = qs[z]
    vmat[HD:, :] = jnp.ones((8, NZ * ROWS), BF16)
    take_kv(z)
    wz_far(1).wait_recv()
    wz_opposite().start()
    wz_far(3).wait_recv()
    issue(PACE[1])
    wz_opposite().wait_recv()
    wz_near(0).start()
    wz_near(1).start()
    issue(PACE[2])
    wz_near(0).wait_recv()
    wz_near(2).start()
    wz_near(1).wait_recv()
    wz_near(3).start()
    issue(PACE[3])
    wz_near(2).wait_recv()
    wz_near(3).wait_recv()
    wx_copy(0).start()
    wy_copy(0).start()
    wy_copy(1).start()
    issue(len(queue))

    kv_copy(8).wait_recv()
    take_kv((z + 8) % NZ)
    lax.fori_loop(1, KV1, lambda i, c: kv_take(8 - i, c), 0)
    wy_copy(0).wait_recv()
    wy_pass(0).start()
    wx_copy(1).start()
    wy_copy(1).wait_recv()
    wy_pass(1).start()
    wx_copy(2).start()
    lax.fori_loop(KV1, 8, lambda i, c: kv_take(8 - i, c), 0)

    def wq_pass(unit, way):
        dev, yy = (yr, y_l) if way == 0 else (yl, y_r)
        if unit < 3:
            return remote(wq.at[yy, unit], wq.at[yy, unit], sqy.at[way, 4 + unit], rqy.at[way, 4 + unit], dev)
        return remote(wo.at[yy], wo.at[yy], sqy.at[way, 7], rqy.at[way, 7], dev)

    def o_copy(i):
        to = (z + i) % NZ
        return remote(osd.at[to], orc.at[z], so.at[i], ro.at[i], {"space": to})

    def attend(i, c):
        d = 8 - i
        src_a = (z + NZ - d) % NZ
        src_b = jnp.where(d == 8, z, (z + d) % NZ)
        q_copy(d).wait_recv()

        @pl.when(d < 8)
        def _():
            q_copy(NZ - d).wait_recv()

        queries = jnp.concatenate([qr[src_a], qr[src_b]], axis=1)
        s = jnp.dot(kmat[...], queries, preferred_element_type=F32)
        top = jnp.max(s, axis=0, keepdims=True)
        p = jnp.exp2((s - top) * FACTOR2).astype(BF16)
        o = jnp.dot(vmat[...], p, preferred_element_type=F32)
        o = (o[:HD] / o[HD : HD + 1]).astype(BF16)
        osd[src_a] = o[:, :ROWS]
        osd[src_b] = o[:, ROWS:]
        o_copy(NZ - d).start()

        @pl.when(d < 8)
        def _():
            o_copy(d).start()

        @pl.when(i == 1)
        def _():
            wy_pass(0).wait_recv()
            wy_pass(1).wait_recv()
            wx_copy(3).start()

        @pl.when(i == 2)
        def _():
            for unit, way in ((0, 0), (2, 1), (1, 0), (3, 1)):
                wq_send(unit, way).wait_recv()
                wq_pass(unit, way).start()

        return c

    lax.fori_loop(0, 8, attend, 0)
    orc[z] = osd[z]

    for i in range(4):
        wx_copy(i).wait_recv()

    def w_rows(i, c):
        m, k = i // 4, i % 4
        for b in range(8):
            wall[i, :, 128 * b : 128 * (b + 1)] = ws[b, m, k, 16:]
        last = [ws[b, m, k, :16].astype(F32) for b in range(5)]
        wall[i, :, 1024:] = jnp.concatenate(last, axis=0)[:HD].astype(BF16)
        return c

    lax.fori_loop(0, NZ, w_rows, 0)

    def project(r):
        slot = (r % 4) * 4 + ((r + 1) // 4) % 4
        return jnp.dot(orc[(z + r) % NZ].astype(F32).T.astype(BF16), wall[slot], preferred_element_type=F32)

    def o_take(i, c):
        d = 8 - i
        o_copy(d).wait_recv()
        o_copy(NZ - d).wait_recv()
        acc[...] += project(NZ - d) + project(d)
        return c

    acc[...] = project(0)
    o_copy(8).wait_recv()
    acc[...] += project(8)
    lax.fori_loop(1, 7, o_take, 0)
    o_copy(1).wait_recv()
    o_copy(NZ - 1).wait_recv()
    loc_h.wait()
    projected = acc[...] + project(NZ - 1) + project(1)
    mids[...] = (hid[...].astype(F32) + gs_ref[...] * projected).astype(BF16)

    def mid_copy(i, part):
        to = (t + i) % NT
        rows = pl.ds(pl.multiple_of((to // 2) * PART + HALF * part, HALF), HALF)
        return remote(mids.at[rows], midr.at[part, t], sm.at[part, i], rm.at[part, i], {"tm": to})

    for part in range(2):
        for i in (5, 3, 1, 7, 4, 2, 6):
            mid_copy(i, part).start()
        midr[part, t] = mids[pl.ds(pl.multiple_of(y * PART + HALF * part, HALF), HALF), :]

    loc_q.wait()
    loc_o.wait()
    for unit, way in ((2, 0), (3, 0), (0, 1), (1, 1)):
        wq_send(unit, way).wait_recv()
    for unit, way in ((0, 0), (2, 1), (1, 0), (3, 1)):
        wq_pass(unit, way).wait_recv()

    tokens = NT * HALF
    same = (lax.broadcasted_iota(jnp.int32, (tokens, tokens), 0) % HALF) == (
        lax.broadcasted_iota(jnp.int32, (tokens, tokens), 1) % HALF
    )
    keep = jnp.where(xh == 0, 1.0, 0.0).astype(F32)
    ones = jnp.ones((8, tokens), F32)

    def fin_copy(f, part):
        return remote(
            fins.at[part, f], finr.at[t, pl.ds(HALF * part, HALF)], sf.at[part, f], rf.at[part, t],
            {"section": nxt, "tm": f},
        )

    for part in range(2):
        for i in range(1, NT):
            mid_copy(i, part).wait_recv()
        middle = midr[part].reshape(tokens, D).astype(F32)
        centred = middle - jnp.mean(middle, axis=-1, keepdims=True)
        variance = jnp.mean(centred * centred, axis=-1, keepdims=True)
        normed = (centred * lax.rsqrt(variance + 1e-06) * (1.0 + sc_ref[...]) + sh_ref[...]).astype(BF16)
        proj[...] = lax.dot_general(
            normed, wq[...].reshape(12 * 144, D), (((1,), (1,)), ((), ())), preferred_element_type=F32
        ).T
        for head in range(8):
            at = 432 * (head // 2) + HD * (head % 2)
            tq = proj[at : at + HD, :].astype(BF16)
            tk = proj[at + 144 : at + 144 + HD].T.astype(BF16)
            tv = jnp.concatenate([proj[at + 288 : at + 288 + HD], ones], axis=0).astype(BF16)
            s = jnp.where(same, jnp.dot(tk, tq, preferred_element_type=F32), -jnp.inf)
            p = jnp.exp2((s - jnp.max(s, axis=0, keepdims=True)) * FACTOR2).astype(BF16)
            o = jnp.dot(tv, p, preferred_element_type=F32)
            mixt[HD * head : HD * (head + 1), :] = o[:HD] / o[HD : HD + 1]
        mixed = mixt[...].T.astype(BF16)
        summed = jnp.dot(mixed, wo[...].reshape(576, D), preferred_element_type=F32)
        done = keep * middle + gt_ref[...] * summed
        fins[part] = done.astype(BF16).reshape(NT, HALF, D)
        for f in range(NT):
            fin_copy(f, part).start()

    def fin_wait(f, c):
        for part in range(2):
            remote(
                fins.at[part, f], finr.at[f, pl.ds(HALF * part, HALF)], sf.at[part, f], rf.at[part, f],
                {"section": nxt, "tm": f},
            ).wait_recv()
        return c

    lax.fori_loop(0, NT, fin_wait, 0)

    def left_z(i, c):
        kv_copy(i).wait_send()
        q_copy(i).wait_send()
        o_copy(i).wait_send()
        return c

    lax.fori_loop(1, NZ, left_z, 0)

    wz_far(1).wait_send()
    wz_far(3).wait_send()
    wz_opposite().wait_send()
    for i in range(4):
        wz_near(i).wait_send()
        wy_copy(i).wait_send() if i < 2 else wy_pass(i - 2).wait_send()
        wx_copy(i).wait_send()
        for way in range(2):
            wq_send(i, way).wait_send()
    for unit, way in ((0, 0), (2, 1), (1, 0), (3, 1)):
        wq_pass(unit, way).wait_send()

    def left_t(i, c):
        mid_copy(i, 0).wait_send()
        mid_copy(i, 1).wait_send()
        return c

    lax.fori_loop(1, NT, left_t, 0)

    def left_f(f, c):
        fin_copy(f, 0).wait_send()
        fin_copy(f, 1).wait_send()
        return c

    lax.fori_loop(0, NT, left_f, 0)


def shards(
    hidden_in, query_s, key_s, value_s, out_proj_s, gate_s, shift_t, scale_t, qkv_t, out_t, gate_t
):
    vm = pl.BlockSpec(memory_space=pltpu.VMEM)
    hbm = pl.BlockSpec(memory_space=pl.ANY)
    dma = pltpu.SemaphoreType.DMA
    plane = (HD, ROWS)
    out = pl.pallas_call(
        kernel,
        out_shape=jax.ShapeDtypeStruct((NT, PART, D), BF16),
        in_specs=[hbm, hbm, hbm, hbm, hbm, vm, vm, vm, hbm, hbm, vm],
        out_specs=hbm,
        scratch_shapes=[
            pltpu.VMEM((ROWS, D), BF16),
            pltpu.VMEM((ROWS, D), BF16),
            pltpu.VMEM((ROWS, D), BF16),
            pltpu.VMEM((HD, D), BF16),
            pltpu.VMEM((NZ, 2 * HD, ROWS), BF16),
            pltpu.VMEM((NZ, 2 * HD, ROWS), BF16),
            pltpu.VMEM((NZ, *plane), BF16),
            pltpu.VMEM((NZ, *plane), BF16),
            pltpu.VMEM((NZ, *plane), BF16),
            pltpu.VMEM((NZ, *plane), BF16),
            pltpu.VMEM((80, 128), BF16),
            pltpu.VMEM((NT, 4, 4, 88, 128), BF16),
            pltpu.VMEM((NZ, HD, D), BF16),
            pltpu.VMEM((ROWS, D), F32),
            pltpu.VMEM((NZ * ROWS, HD), BF16),
            pltpu.VMEM((HD + 8, NZ * ROWS), BF16),
            pltpu.VMEM((4, 3, 144, D), BF16),
            pltpu.VMEM((4, 144, D), BF16),
            pltpu.VMEM((ROWS, D), BF16),
            pltpu.VMEM((ROWS, D), BF16),
            pltpu.VMEM((2, NT, HALF, D), BF16),
            pltpu.VMEM((1728, NT * HALF), F32),
            pltpu.VMEM((576, NT * HALF), F32),
            pltpu.VMEM((2, NT, HALF, D), BF16),
            dma((NZ,)), dma((NZ,)), dma((NZ,)), dma((NZ,)), dma((NZ,)), dma((NZ,)),
            dma((8,)), dma((8,)), dma((4,)), dma((4,)), dma((4,)), dma((4,)),
            dma((2, 8)), dma((2, 8)), dma((2, NT)), dma((2, NT)), dma((2, NT)), dma((2, NT)), dma((7,)),
        ],
        compiler_params=pltpu.CompilerParams(
            collective_id=0, has_side_effects=True, vmem_limit_bytes=56 * 1024 * 1024
        ),
        cost_estimate=pl.CostEstimate(flops=3_000_000_000, bytes_accessed=6_000_000, transcendentals=4_500_000),
        name="st_block_pair",
    )(
        query_s[0, 0], key_s[0, 0], value_s[0, 0], hidden_in[0, 0], out_proj_s[0],
        gate_s, shift_t, scale_t, qkv_t[0], out_t[0], gate_t,
    )
    halves = out.reshape(4, 2, PART, D)
    return (halves[:, 0] + halves[:, 1]).reshape(1, 1, ROWS, D)


def solution(mesh):
    in_specs = (
        P("section", "tm", "space", None),
        P("section", "tm", "space", None),
        P("section", "tm", "space", None),
        P("section", "tm", "space", None),
        P("section", "space", None),
        P("section", None),
        P("section", None),
        P("section", None),
        P("section", None, "tm", None),
        P("section", "tm", None),
        P("section", None),
    )
    out_specs = P("section", "tm", "space", None)
    return jax.shard_map(shards, mesh=mesh, in_specs=in_specs, out_specs=out_specs, check_vma=False)
```
